1024 devices in a mesh: ctx: 64 (over z, x), ep: 16 (over y, core).
Axes of the slice: x: 4, y: 8, z: 16, core: 2. Of those that a mesh axis runs over, the one named last changes fastest.
Arguments:
- grad_out: bfloat16 [8192, 6144], P('ctx', 'ep'), may hold values from -24 to 24
- logits: float32 [8192, 16], P('ctx'), may hold values from -8 to 270
- expert_ids: int32 [8192, 4], P('ctx'), may hold values from 0 to 15, as said below
- hidden_act: bfloat16 [10752, 3328], P('ctx'), may hold values from -1.5 to 1.5
- down_weight: bfloat16 [10752, 6144], P('ctx', 'ep'), may hold values from -0.0625 to 0.0625
- router_weight: float32 [6144, 16], P('ep'), may hold values from -0.3 to 0.3
Outputs:
- grad_down: bfloat16 [10752, 6144], P('ctx', 'ep')
- grad_hidden: bfloat16 [10752, 3328], P('ctx', 'ep')
- grad_tokens: bfloat16 [8192, 6144], P('ctx', 'ep')
The draws below stay inside these ranges and needn't reach their ends.
Inputs may be any that keep to these rules, and one draw needn't show every extreme that they name: `expert_ids`: each token names 4 different experts. Within each block of 128 tokens (the tokens of one index of ctx) the tokens that name expert 0 number at least a quarter of 52, rounded down, and at most 52, and in every draw some block has exactly 52 of them.
All inputs are finite; a program needn't handle non-finite values.
Results may differ from the reference program's by a relative error of at most 0.0057.
Values may be sent and summed in bfloat16 or wider, within the bound.
A program may use at most 32 MiB of HBM per device.

```python
import jax
import jax.numpy as jnp
from jax import lax

D = 6144
FF = 10752
EXPERTS = 16
TOP = 4
TOK_CTX = 128
TOKENS = 8192
CAP = 52
SLOTS = 3328
N_CTX = 64


def draw_logits(key, part):
    key = jax.random.fold_in(key, 11)
    values = 2.0 * jax.random.normal(key, (TOKENS, EXPERTS), jnp.float32)
    return jnp.clip(values, -8.0, 8.0).astype(jnp.float32)


def draw_expert_ids(key, part):
    key = jax.random.fold_in(key, 23)
    count_key, full_key, token_key, other_key, column_key = jax.random.split(key, 5)
    counts = jax.random.randint(count_key, (N_CTX,), CAP // 4, CAP + 1)
    full_block = jax.random.randint(full_key, (), 0, N_CTX)
    counts = jnp.where(jnp.arange(N_CTX, dtype=jnp.int32) == full_block, CAP, counts)
    token_scores = jax.random.randint(token_key, (N_CTX, TOK_CTX), 0, 1 << 20) * TOK_CTX + jnp.arange(TOK_CTX, dtype=jnp.int32)[None, :]
    ordering = jnp.argsort(token_scores, axis=1)
    ranking = jnp.argsort(ordering, axis=1)
    is_named = (ranking < counts[:, None]).reshape(TOKENS, 1)
    other_scores = jax.random.randint(other_key, (TOKENS, EXPERTS - 1), 0, 1 << 20) * (EXPERTS - 1) + jnp.arange(EXPERTS - 1, dtype=jnp.int32)[None, :]
    picked = jnp.argsort(other_scores, axis=1)[:, :TOP].astype(jnp.int32) + 1
    column = jax.random.randint(column_key, (TOKENS, 1), 0, TOP)
    slot_column = jnp.arange(TOP, dtype=jnp.int32)[None, :] == column
    return jnp.where(is_named & slot_column, 0, picked).astype(jnp.int32)


def shard_levels(rng, shape, cuts, low, top_value):
    gain = 1.0
    for axis_at, shards_of in cuts:
        steps = jax.random.uniform(jax.random.fold_in(jax.random.fold_in(rng, 6), axis_at), (shards_of,), jnp.float32, low / len(cuts), top_value / len(cuts))
        gain = gain * jnp.repeat(jnp.exp(steps), shape[axis_at] // shards_of).reshape((-1,) + (1,) * (len(shape) - 1 - axis_at))
    return gain


def bell_draw(stream_key, dims, scale, limit, cuts=(), held_as=jnp.bfloat16):
    entries = scale * jax.random.normal(stream_key, dims, jnp.float32)
    if cuts:
        entries = entries * shard_levels(stream_key, dims, cuts, -0.22, 0.18)
    return jnp.clip(entries, -limit, limit).astype(held_as)


def setup_inputs(seed: int = 0) -> dict:
    key_list = jax.random.split(jax.random.key(seed), 7)
    grad_out = bell_draw(key_list[0], (TOKENS, D), 4.0, 24.0, ((0, 64), (1, 16)))
    logits = draw_logits(jax.random.fold_in(key_list[6], 71), 0)
    expert_ids = draw_expert_ids(jax.random.fold_in(key_list[6], 71), 0)
    hidden_act = bell_draw(key_list[3], (FF, SLOTS), 0.25, 1.5, ((0, 64),))
    down_weight = bell_draw(key_list[4], (FF, D), FF ** -0.5, 0.0625, ((0, 64), (1, 16)))
    router_weight = bell_draw(key_list[5], (D, EXPERTS), 0.05, 0.3, ((0, 16),), jnp.float32)
    return dict(grad_out=grad_out, logits=logits, expert_ids=expert_ids, hidden_act=hidden_act, down_weight=down_weight, router_weight=router_weight)


def reference(grad_out, logits, expert_ids, hidden_act, down_weight, router_weight):
    router_probs = jax.nn.softmax(logits.astype(jnp.float32), axis=-1)
    is_named = jnp.any(expert_ids == 0, axis=1)
    route_weight = jnp.where(is_named, router_probs[:, 0], 0.0).astype(jnp.bfloat16)
    named_blocks = is_named.reshape(N_CTX, TOK_CTX)
    named_count = named_blocks.astype(jnp.float32)
    slot_pos = (jnp.cumsum(named_count, axis=1) - named_count).astype(jnp.int32)
    slots_iota = jnp.arange(CAP, dtype=jnp.int32)
    select = jnp.where(named_blocks[:, :, None] & (slot_pos[:, :, None] == slots_iota[None, None, :]), 1.0, 0.0).astype(jnp.float32)
    token_blocks = grad_out.astype(jnp.float32).reshape(N_CTX, TOK_CTX, D)
    slot_grad = jnp.einsum('stj,std->sjd', select, token_blocks, precision=lax.Precision.HIGHEST).reshape(SLOTS, D).astype(jnp.bfloat16)
    weight_blocks = route_weight.astype(jnp.float32).reshape(N_CTX, TOK_CTX)
    slot_weight = jnp.einsum('stj,st->sj', select, weight_blocks, precision=lax.Precision.HIGHEST).reshape(SLOTS).astype(jnp.bfloat16)
    weights = slot_weight.astype(jnp.float32)
    scaled = (weights[:, None] * slot_grad.astype(jnp.float32)).astype(jnp.bfloat16)
    grad_down = jnp.dot(hidden_act, scaled, preferred_element_type=jnp.float32).astype(jnp.bfloat16)
    backward = lax.dot_general(slot_grad, down_weight, (((1,), (1,)), ((), ())), preferred_element_type=jnp.float32)
    grad_hidden = (weights[:, None] * backward).astype(jnp.bfloat16).T
    slot_score = jnp.sum(hidden_act.astype(jnp.float32).T * backward, axis=1)
    flat_pos = (jnp.arange(N_CTX, dtype=jnp.int32)[:, None] * CAP + slot_pos).reshape(TOKENS)
    route_grad = jnp.where(is_named, slot_score[flat_pos], 0.0)
    spread = jnp.where(jnp.arange(EXPERTS, dtype=jnp.int32)[None, :] == 0, route_grad[:, None], 0.0)
    logit_grad = router_probs * (spread - jnp.sum(router_probs * spread, axis=1, keepdims=True))
    grad_tokens = jnp.dot(logit_grad, router_weight.T, precision=lax.Precision.HIGHEST).astype(jnp.bfloat16)
    return grad_down, grad_hidden, grad_tokens
```

```python
import functools

import jax
import jax.numpy as jnp
from jax import lax
from jax.experimental import pallas as pl
from jax.experimental.pallas import tpu as pltpu
from jax.sharding import PartitionSpec as P

MESH = pl.DeviceIdType.MESH
CAP = 52
NZ, NX, NY = 16, 4, 8
DZ = (0, 1, -1, 3, -3, 2, -2, 4, -4, 6, -6, 5, -5, 7, -7, 8)
AT = {d: i for i, d in enumerate(DZ)}
AT[-8] = AT[8]
GROUPS = ((0, 5), (5, 11), (11, 16))
HAND_ON = {
    0: (3, -3, 1, -1),
    -3: (3, 1, -1),
    3: (-3, 1, -1),
    -6: (1, -1, 2),
    6: (1, -1),
}
F32, BF16 = jnp.float32, jnp.bfloat16


def pick(index, table):
    out = jnp.int32(table[0])
    for i, v in enumerate(table):
        if i:
            out = jnp.where(index == i, jnp.int32(v), out)
    return out


def kernel(
    grad_out, logits_t, ids_t, hidden, down, router_t,
    grad_down, grad_hidden, grad_tokens,
    go_v, log_v, ids_v, hid_v, down_v, rw_v,
    hp, wp, abuf, bbuf, acc, own, pbuf, sib, comb, rsb, wshare,
    sc, s1, s2s, s2, s3s, s3, s4s, s4, sel_t, qmat,
    in_sem, ax_s, ax_r, az_s, az_r, bz_s, bz_r, bx_s, bx_r,
    sib_s, sib_r, y_s, y_r, s1_s, s1_r, s2_s, s2_r, s3_s, s3_r, s4_s, s4_r,
):
    ctx, ep = lax.axis_index("ctx"), lax.axis_index("ep")
    z, x = ctx // NX, lax.rem(ctx, NX)
    y, core = ep // 2, lax.rem(ep, 2)

    def at_z(d):
        return (lax.rem(z + d + NZ, NZ) * NX + x, ep)

    def at_x(d):
        return (z * NX + lax.rem(x + d, NX), ep)

    def at_y(d):
        return (ctx, lax.rem(y + d, NY) * 2 + core)

    sibling = (ctx, y * 2 + 1 - core)

    def remote(src, dst, send, recv, to):
        return pltpu.make_async_remote_copy(
            src_ref=src, dst_ref=dst, send_sem=send, recv_sem=recv, device_id=to, device_id_type=MESH
        )

    loads = [
        pltpu.make_async_copy(s, d, in_sem.at[i])
        for i, (s, d) in enumerate(
            ((ids_t, ids_v), (grad_out, go_v), (logits_t, log_v), (hidden, hid_v), (down, down_v), (router_t, rw_v))
        )
    ]
    for c in loads:
        c.start()

    barrier = pltpu.get_barrier_semaphore()
    greet = [at_z(d) for d in (1, -1, 2, -2, 3, -3)] + [at_x(d) for d in (1, 2, 3)]
    greet += [at_y(d) for d in range(1, NY)] + [sibling]
    for to in greet:
        pl.semaphore_signal(barrier, inc=1, device_id=to, device_id_type=MESH)

    loads[0].wait()
    named = jnp.max(jnp.where(ids_v[...] == 0, 1.0, 0.0).astype(F32), axis=0, keepdims=True)
    rows = lax.broadcasted_iota(jnp.int32, (128, 128), 0)
    cols = lax.broadcasted_iota(jnp.int32, (128, 128), 1)
    before = jnp.where(rows < cols, 1.0, 0.0).astype(BF16)
    named8 = jnp.broadcast_to(named, (8, 128))
    pos = jnp.dot(named8.astype(BF16), before, preferred_element_type=F32)[0:1]
    slot_row = lax.rem(rows, 64).astype(F32)
    sel = jnp.where((slot_row == pos) & (named > 0.5), 1.0, 0.0).astype(F32)
    sel_bf = sel.astype(BF16)

    loads[2].wait()
    logit = log_v[...]
    grown = jnp.exp(logit - jnp.max(logit, axis=0, keepdims=True))
    probs = grown / jnp.sum(grown, axis=0, keepdims=True)
    p0 = probs[0:1]
    weight = jnp.where(named > 0.5, p0, 0.0).astype(BF16)
    weight_row = lax.dot_general(
        jnp.broadcast_to(weight.astype(F32), (8, 128)).astype(BF16), sel_bf,
        (((1,), (1,)), ((), ())), preferred_element_type=F32,
    )[0:1]

    loads[1].wait()
    slots = jnp.dot(sel_bf[0:64], go_v[...], preferred_element_type=F32)
    row64 = lax.broadcasted_iota(jnp.int32, (64, 128), 0)
    abuf[0, x] = jnp.where(row64 == CAP, weight_row, slots[:, 0:128]).astype(BF16)
    bbuf[x, 0] = jnp.concatenate([slots[0:56, 128:256], slots[0:56, 256:384]], axis=0).astype(BF16)

    pl.semaphore_wait(barrier, len(greet))

    sends = []

    def start(c):
        c.start()
        sends.append(c)

    ax_in = []
    for d in (1, 3, 2):
        start(remote(abuf.at[0, x], abuf.at[0, x], ax_s.at[d], ax_r.at[d], at_x(d)))

    az_in, bz_in = {}, {}

    def hand_on(buf_of, d, send, recv, into, base):
        for i, shift in enumerate(HAND_ON[d]):
            there = AT[d - shift]
            c = remote(buf_of(AT[d]), buf_of(there), send.at[base + i], recv.at[there], at_z(shift))
            start(c)
            into[there] = c

    bases = {0: 0, -3: 4, 3: 7, -6: 10, 6: 13}

    def send_a(d):
        hand_on(lambda i: abuf.at[i], d, az_s, az_r, az_in, bases[d])

    def send_b(d):
        hand_on(lambda i: bbuf.at[x, i], d, bz_s, bz_r, bz_in, bases[d])

    def wait_a(d):
        i = AT[d]
        remote(abuf.at[i], abuf.at[i], az_s.at[0], az_r.at[i], at_z(1)).wait_recv()

    def wait_b(d):
        i = AT[d]
        remote(bbuf.at[x, i], bbuf.at[x, i], bz_s.at[0], bz_r.at[i], at_z(1)).wait_recv()

    def send_bx(g):
        lo, hi = GROUPS[g]
        for d in (1, 3, 2):
            block = bbuf.at[x, pl.ds(lo, hi - lo)]
            start(remote(block, block, bx_s.at[g, d], bx_r.at[g, d], at_x(d)))

    def wait_bx(g):
        lo, hi = GROUPS[g]
        for d in (1, 3, 2):
            block = bbuf.at[lax.rem(x + NX - d, NX), pl.ds(lo, hi - lo)]
            remote(block, block, bx_s.at[g, d], bx_r.at[g, d], at_x(d)).wait_recv()

    send_b(0)

    loads[4].wait()
    zero8 = jnp.zeros((8, 384), F32)
    wp[...] = jnp.concatenate([down_v[...].astype(F32), zero8], axis=0).astype(BF16)
    loads[3].wait()

    def spread(e, _):
        first = e * (NX * CAP)
        tile = jnp.minimum(first // 128, 23)
        off = first - tile * 128
        r = lax.broadcasted_iota(jnp.int32, (384, 256), 0)
        c = lax.broadcasted_iota(jnp.int32, (384, 256), 1)
        lane = lax.rem(c, 64)
        move = jnp.where((r == off + (c // 64) * CAP + lane) & (lane < CAP), 1.0, 0.0).astype(BF16)
        out = jnp.dot(hid_v[:, pl.ds(pl.multiple_of(tile * 128, 128), 384)], move, preferred_element_type=F32)
        hp[e] = jnp.concatenate([out, jnp.zeros((8, 256), F32)], axis=0).astype(BF16)
        return 0

    lax.fori_loop(0, 6, spread, 0)

    for d in (1, 3, 2):
        block = abuf.at[0, lax.rem(x + NX - d, NX)]
        remote(block, block, ax_s.at[d], ax_r.at[d], at_x(d)).wait_recv()
    send_a(0)

    lax.fori_loop(6, 16, spread, 0)
    acc[...] = jnp.zeros_like(acc)

    wait_b(-3)
    send_b(-3)
    wait_b(3)
    send_b(3)
    wait_b(1)
    wait_b(-1)
    send_bx(0)
    wait_a(-3)
    send_a(-3)
    wait_a(3)
    send_a(3)

    sel_t[...] = sel.T
    loads[5].wait()
    slope = probs * (jnp.where(lax.broadcasted_iota(jnp.int32, (16, 128), 0) == 0, 1.0, 0.0) - p0)
    qmat[...] = lax.dot_general(
        slope, rw_v[...], (((0,), (0,)), ((), ())), precision=lax.Precision.HIGHEST, preferred_element_type=F32
    )

    wait_b(-6)
    send_b(-6)
    wait_b(6)
    send_b(6)
    for d in (2, -2, 4, -4):
        wait_b(d)
    send_bx(1)
    wait_a(-6)
    send_a(-6)
    wait_a(6)
    send_a(6)

    lane128 = lax.broadcasted_iota(jnp.int32, (1, 128), 1)
    row8 = lax.broadcasted_iota(jnp.int32, (8, 128), 0)

    def share_of(i):
        return lax.rem(z + pick(i, DZ) + NZ, NZ)

    def to_owner(i):
        e = share_of(i)
        return remote(sc.at[i], s1.at[i], s1_s.at[i], s1_r.at[i], (e * NX + x, ep))

    def to_sibling(i):
        return remote(pbuf.at[i], sib.at[i], sib_s.at[i], sib_r.at[i], sibling)

    def to_share(i):
        e = share_of(i)
        return remote(comb.at[i], rsb.at[y], y_s.at[i], y_r.at[y], (ctx, e))

    def add_pair(i):
        e = share_of(i)

        @pl.when(lax.rem(e, 2) == core)
        def _():
            to_sibling(i).wait_recv()
            both = (own[lax.rem(i, 2)] + sib[i].astype(F32)).astype(BF16)

            @pl.when(e == ep)
            def _():
                rsb[y] = both

            @pl.when(e != ep)
            def _():
                comb[i] = both
                to_share(i).start()

    def chunk(i, _):
        e = share_of(i)
        a = [abuf[i, k].astype(F32) for k in range(NX)]
        b = [bbuf[k, i].astype(F32) for k in range(NX)]
        pad = jnp.zeros((8, 128), F32)
        g0 = jnp.concatenate(a, axis=0).astype(BF16)
        g1 = jnp.concatenate([v for k in range(NX) for v in (b[k][0:56], pad)], axis=0).astype(BF16)
        g2 = jnp.concatenate([v for k in range(NX) for v in (b[k][56:112], pad)], axis=0).astype(BF16)
        g = jnp.concatenate([g0, g1, g2], axis=1)
        w = jnp.concatenate(
            [jnp.where(lane128 < 64, a[k][CAP:CAP + 1], a[k + 1][CAP:CAP + 1]) for k in (0, 2)], axis=1
        )
        h = hp[e].astype(F32)
        back = lax.dot_general(wp[...], g, (((1,), (1,)), ((), ())), preferred_element_type=F32)
        score = jnp.sum(h * back, axis=0, keepdims=True)
        both_rows = jnp.where(row8 == 0, score[:, 0:128], jnp.where(row8 == 1, score[:, 128:256], 0.0))

        @pl.when(i == 0)
        def _():
            s1[0] = both_rows

        @pl.when(i != 0)
        def _():
            sc[i] = both_rows
            to_owner(i).start()

        @pl.when(lax.rem(e, 2) == core)
        def _():
            own[lax.rem(i, 2)] = back

        @pl.when(lax.rem(e, 2) != core)
        def _():
            pbuf[i] = back.astype(BF16)
            to_sibling(i).start()

        @pl.when(e == ep)
        def _():
            wshare[...] = jnp.broadcast_to(w, (8, 256))

        acc[...] += jnp.dot((h * w).astype(BF16), g, preferred_element_type=F32)

        @pl.when(i != 0)
        def _():
            add_pair(i - 1)

        return 0

    for d in (1, -1):
        wait_a(d)
    wait_bx(0)
    lax.fori_loop(0, 2, chunk, 0)
    for d in (5, -5, 7, -7, 8):
        wait_b(d)
    send_bx(2)
    lax.fori_loop(2, 5, chunk, 0)
    for d in (2, -2, 4, -4):
        wait_a(d)
    wait_bx(1)
    lax.fori_loop(5, 11, chunk, 0)
    for d in (5, -5, 7, -7, 8):
        wait_a(d)
    wait_bx(2)
    lax.fori_loop(11, 16, chunk, 0)
    add_pair(15)

    def s1_wait(i, _):
        to_owner(i).wait_recv()
        return 0

    grad_down[...] = acc[0:168].astype(BF16)
    lax.fori_loop(1, 16, s1_wait, 0)
    s2s[...] = jnp.sum(s1[...], axis=0)
    for d in (1, 3, 2):
        start(remote(s2s, s2.at[d], s2_s.at[d], s2_r.at[d], at_x(d)))
    s2[0] = s2s[...]
    for d in (1, 3, 2):
        remote(s2s, s2.at[d], s2_s.at[d], s2_r.at[d], at_x(d)).wait_recv()
    s3s[...] = jnp.sum(s2[...], axis=0)
    for d in range(1, NY):
        start(remote(s3s, s3.at[d], s3_s.at[d], s3_r.at[d], at_y(d)))
    s3[0] = s3s[...]

    for d in range(1, NY):
        src = lax.rem(y + NY - d, NY)
        remote(rsb.at[src], rsb.at[src], y_s.at[0], y_r.at[src], sibling).wait_recv()
    total = rsb[0].astype(F32)
    for d in range(1, NY):
        total = total + rsb[d].astype(F32)
    total = total * wshare[0:1]
    grad_hidden[...] = jnp.concatenate(
        [total[0:168, 64 * k:64 * k + CAP] for k in range(NX)], axis=1
    ).astype(BF16)

    for d in range(1, NY):
        remote(s3s, s3.at[d], s3_s.at[d], s3_r.at[d], at_y(d)).wait_recv()
    s4s[...] = jnp.sum(s3[...], axis=0)
    start(remote(s4s, s4, s4_s.at[0], s4_r.at[0], sibling))
    remote(s4s, s4, s4_s.at[0], s4_r.at[0], sibling).wait_recv()
    scores = s4s[...] + s4[...]
    row = jnp.where(x >= 2, scores[1:2], scores[0:1])
    row = jnp.where(lane128 // 64 == lax.rem(x, 2), row, 0.0)
    route = jnp.sum(sel_t[...] * row, axis=1, keepdims=True)
    grad_tokens[...] = (route * qmat[...]).astype(BF16)

    for c in sends:
        c.wait_send()

    def drain(i, _):
        @pl.when(i != 0)
        def _():
            to_owner(i).wait_send()

        e = share_of(i)

        @pl.when(lax.rem(e, 2) != core)
        def _():
            to_sibling(i).wait_send()

        @pl.when((lax.rem(e, 2) == core) & (e != ep))
        def _():
            to_share(i).wait_send()

        return 0

    lax.fori_loop(0, 16, drain, 0)


def shards(grad_out, logits, expert_ids, hidden_act, down_weight, router_weight):
    dma = pltpu.SemaphoreType.DMA
    ng = len(GROUPS)
    return pl.pallas_call(
        kernel,
        out_shape=(
            jax.ShapeDtypeStruct((168, 384), BF16),
            jax.ShapeDtypeStruct((168, 208), BF16),
            jax.ShapeDtypeStruct((128, 384), BF16),
        ),
        in_specs=[pl.BlockSpec(memory_space=pl.ANY)] * 6,
        out_specs=[pl.BlockSpec(memory_space=pltpu.VMEM)] * 3,
        scratch_shapes=[
            pltpu.VMEM((128, 384), BF16),
            pltpu.VMEM((16, 128), F32),
            pltpu.VMEM((4, 128), jnp.int32),
            pltpu.VMEM((168, 3328), BF16),
            pltpu.VMEM((168, 384), BF16),
            pltpu.VMEM((16, 384), F32),
            pltpu.VMEM((16, 176, 256), BF16),
            pltpu.VMEM((176, 384), BF16),
            pltpu.VMEM((16, NX, 64, 128), BF16),
            pltpu.VMEM((NX, 16, 112, 128), BF16),
            pltpu.VMEM((176, 384), F32),
            pltpu.VMEM((2, 176, 256), F32),
            pltpu.VMEM((16, 176, 256), BF16),
            pltpu.VMEM((16, 176, 256), BF16),
            pltpu.VMEM((16, 176, 256), BF16),
            pltpu.VMEM((NY, 176, 256), BF16),
            pltpu.VMEM((8, 256), F32),
            pltpu.VMEM((16, 8, 128), F32),
            pltpu.VMEM((16, 8, 128), F32),
            pltpu.VMEM((8, 128), F32),
            pltpu.VMEM((NX, 8, 128), F32),
            pltpu.VMEM((8, 128), F32),
            pltpu.VMEM((NY, 8, 128), F32),
            pltpu.VMEM((8, 128), F32),
            pltpu.VMEM((8, 128), F32),
            pltpu.VMEM((128, 128), F32),
            pltpu.VMEM((128, 384), F32),
            dma((6,)),
            dma((NX,)), dma((NX,)),
            dma((15,)), dma((16,)),
            dma((15,)), dma((16,)),
            dma((ng, NX)), dma((ng, NX)),
            dma((16,)), dma((16,)),
            dma((16,)), dma((NY,)),
            dma((16,)), dma((16,)),
            dma((NX,)), dma((NX,)),
            dma((NY,)), dma((NY,)),
            dma((1,)), dma((1,)),
        ],
        compiler_params=pltpu.CompilerParams(
            collective_id=0, has_side_effects=True, vmem_limit_bytes=48 << 20
        ),
    )(grad_out, logits.T, expert_ids.T, hidden_act, down_weight, router_weight.T)


def solution(mesh):
    placed = (
        P("ctx", "ep"),
        P("ctx", None),
        P("ctx", None),
        P("ctx", None),
        P("ctx", "ep"),
        P("ep", None),
    )
    return jax.shard_map(
        shards,
        mesh=mesh,
        in_specs=placed,
        out_specs=(P("ctx", "ep"), P("ctx", "ep"), P("ctx", "ep")),
        check_vma=False,
    )
```

```python
import functools

import jax
import jax.numpy as jnp
from jax import lax
from jax.experimental import pallas as pl
from jax.experimental.pallas import tpu as pltpu
from jax.sharding import PartitionSpec as P

MESH = pl.DeviceIdType.MESH
CAP = 52
NZ, NX, NY = 16, 4, 8
PLAN = (
    (0, ((0, 0, 1), (0, 0, 3), (0, 0, 2), (2, -1, 0), (2, 1, 0))),
    (-1, ((2, -3, 0), (2, 3, 0), (1, -2, 0), (1, 2, 0), (1, -2, 1), (1, 2, 1), (1, -2, 3), (1, 2, 3), (1, -2, 2), (1, 2, 2), (2, -2, 0))),
    (1, ()),
    (-2, ((2, -4, 0), (2, 2, 0), (2, 4, 0), (2, -6, 0), (2, 6, 0), (1, -4, 0), (1, 4, 0), (1, -4, 1), (1, 4, 1))),
    (-3, ((1, -4, 3), (1, 4, 3), (1, -4, 2), (1, 4, 2), (2, -7, 0), (2, -5, 0), (2, 5, 0), (2, 7, 0))),
    (3, ()),
    (-4, ((1, -6, 0), (1, 6, 0), (1, -6, 1), (1, 6, 1))),
    (2, ((1, -6, 3), (1, 6, 3))),
    (4, ((1, -6, 2), (2, 8, 0), (1, 6, 2))),
    (-6, ()),
    (6, ()),
    (-5, ()),
    (-7, ()),
    (5, ()),
    (7, ()),
    (8, ()),
)
DZ = tuple(d for d, _ in PLAN)
AT = {d: i for i, d in enumerate(DZ)}
AT[-8] = AT[8]
HAND_A = {0: (2, -2, 1, -1), -2: (2, 1), 2: (-2, -1), -4: (2, 1), 4: (-2, -1), -6: (1, 2), 6: (-1,)}
HAND_B = {0: (3, -3, 1, -1), -3: (3, 1, -1), 3: (-3, 1, -1), -6: (1, -1), 6: (1, -1), -7: (1,)}
AHEAD = 5
F32, BF16 = jnp.float32, jnp.bfloat16


def pick(index, table):
    out = jnp.int32(table[0])
    for i, v in enumerate(table):
        if i:
            out = jnp.where(index == i, jnp.int32(v), out)
    return out


def pack(v):
    lane = lax.rem(lax.broadcasted_iota(jnp.int32, (144, 256), 1), 64)
    tail = [pltpu.roll(v[144:168], CAP - 12 * c, 1) for c in range(5)]
    tail.append(jnp.zeros((24, 256), F32))
    return jnp.where(lane < CAP, v[0:144], jnp.concatenate(tail, axis=0))


def unpack(v):
    lane = lax.rem(lax.broadcasted_iota(jnp.int32, (24, 256), 1), 64)
    tail = jnp.zeros((24, 256), F32)
    for c in range(5):
        part = pltpu.roll(v[24 * c:24 * c + 24], 256 - (CAP - 12 * c), 1)
        tail = jnp.where((lane >= 12 * c) & (lane < 12 * c + 12), part, tail)
    return jnp.concatenate([v, tail], axis=0)


def kernel(
    grad_out, logits_t, ids_t, hidden, down, router_t,
    grad_down, grad_hidden, grad_tokens,
    go_v, log_v, ids_v, hid_v, down_v, rw_v,
    hp, abuf, bbuf, acc, own, pbuf, sib, comb, rsb, wshare,
    sc, s1, s3s, s3, s4s, s4, sel_t, qmat,
    in_sem, ax_s, ax_r, az_s, az_r, bz_s, bz_r, bx_s, bx_r,
    sib_s, sib_r, y_s, y_r, s1_s, s1_r, s3_s, s3_r, s4_s, s4_r,
):
    ctx, ep = lax.axis_index("ctx"), lax.axis_index("ep")
    z, x = ctx // NX, lax.rem(ctx, NX)
    y, core = ep // 2, lax.rem(ep, 2)

    def at_z(d):
        return (lax.rem(z + d + NZ, NZ) * NX + x, ep)

    def at_x(d):
        return (z * NX + lax.rem(x + d, NX), ep)

    def at_y(d):
        return (ctx, lax.rem(y + d, NY) * 2 + core)

    def from_x(o):
        return lax.rem(x + NX - o, NX)

    sibling = (ctx, y * 2 + 1 - core)

    def remote(src, dst, send, recv, to):
        return pltpu.make_async_remote_copy(
            src_ref=src, dst_ref=dst, send_sem=send, recv_sem=recv, device_id=to, device_id_type=MESH
        )

    def arrived(ref, sem):
        remote(ref, ref, s4_s, sem, sibling).wait_recv()

    def sent(ref, sem):
        remote(ref, ref, sem, s4_r, sibling).wait_send()

    loads = [
        pltpu.make_async_copy(s, d, in_sem.at[i])
        for i, (s, d) in enumerate(
            ((ids_t, ids_v), (grad_out, go_v), (logits_t, log_v), (hidden, hid_v), (down, down_v), (router_t, rw_v))
        )
    ]
    for c in loads:
        c.start()

    barrier = pltpu.get_barrier_semaphore()
    greet = [at_z(d) for d in (1, -1, 2, -2, 3, -3)] + [at_x(d) for d in (1, 2, 3)]
    greet += [at_y(d) for d in range(1, NY)] + [sibling]
    for to in greet:
        pl.semaphore_signal(barrier, inc=1, device_id=to, device_id_type=MESH)

    loads[0].wait()
    named = jnp.max(jnp.where(ids_v[...] == 0, 1.0, 0.0).astype(F32), axis=0, keepdims=True)
    rows = lax.broadcasted_iota(jnp.int32, (128, 128), 0)
    cols = lax.broadcasted_iota(jnp.int32, (128, 128), 1)
    before = jnp.where(rows < cols, 1.0, 0.0).astype(BF16)
    named8 = jnp.broadcast_to(named, (8, 128))
    pos = jnp.dot(named8.astype(BF16), before, preferred_element_type=F32)[0:1]
    slot_row = lax.rem(rows, 64).astype(F32)
    sel = jnp.where((slot_row == pos) & (named > 0.5), 1.0, 0.0).astype(F32)
    sel_bf = sel.astype(BF16)

    loads[2].wait()
    logit = log_v[...]
    grown = jnp.exp(logit - jnp.max(logit, axis=0, keepdims=True))
    probs = grown / jnp.sum(grown, axis=0, keepdims=True)
    p0 = probs[0:1]
    weight = jnp.where(named > 0.5, p0, 0.0).astype(BF16)
    weight_row = lax.dot_general(
        jnp.broadcast_to(weight.astype(F32), (8, 128)).astype(BF16), sel_bf,
        (((1,), (1,)), ((), ())), preferred_element_type=F32,
    )[0:1]

    loads[1].wait()
    slots = jnp.dot(sel_bf[0:64], go_v[...], preferred_element_type=F32)[0:56]
    row56 = lax.broadcasted_iota(jnp.int32, (56, 128), 0)
    first = jnp.where(row56 == CAP, weight_row, slots[:, 0:128])
    abuf[0, x] = first.reshape(7, 8, 128).astype(BF16)
    bbuf[x, 0] = jnp.concatenate([slots[:, 128:256], slots[:, 256:384]], axis=0).astype(BF16)

    pl.semaphore_wait(barrier, len(greet))

    def leaf(d):
        return d not in HAND_A

    def send_a(d, o):
        k = from_x(o)
        for shift in HAND_A[d]:
            there = d - shift
            if there == -8:
                there = 8
            sem = az_r.at[AT[there], 0 if leaf(there) else o]
            remote(abuf.at[AT[d], k], abuf.at[AT[there], k], az_s, sem, at_z(shift)).start()

    def send_b(d):
        for shift in HAND_B.get(d, ()):
            there = AT[d - shift]
            remote(bbuf.at[x, AT[d]], bbuf.at[x, there], bz_s, bz_r.at[there], at_z(shift)).start()

    def send_bx(i):
        for o in (1, 3, 2):
            remote(bbuf.at[x, i], bbuf.at[x, i], bx_s, bx_r.at[i], at_x(o)).start()

    for o in (1, 3, 2):
        remote(abuf.at[0, x], abuf.at[0, x], ax_s, ax_r.at[o], at_x(o)).start()
    send_b(0)
    send_a(0, 0)
    send_bx(0)

    def hand_on(op, d, o):
        if op == 0:
            arrived(abuf.at[0, from_x(o)], ax_r.at[o])
            send_a(0, o)
        elif op == 1:
            arrived(abuf.at[AT[d], from_x(o)], az_r.at[AT[d], o])
            send_a(d, o)
        else:
            arrived(bbuf.at[x, AT[d]], bz_r.at[AT[d]])
            send_b(d)
            send_bx(AT[d])

    loads[3].wait()

    def share_of(i):
        return lax.rem(z + pick(i, DZ) + NZ, NZ)

    def spread(i, _):
        start = share_of(i) * (NX * CAP)
        tile = jnp.minimum(start // 128, 23)
        off = start - tile * 128
        r = lax.broadcasted_iota(jnp.int32, (384, 256), 0)
        c = lax.broadcasted_iota(jnp.int32, (384, 256), 1)
        lane = lax.rem(c, 64)
        move = jnp.where((r == off + (c // 64) * CAP + lane) & (lane < CAP), 1.0, 0.0).astype(BF16)
        out = jnp.dot(hid_v[:, pl.ds(pl.multiple_of(tile * 128, 128), 384)], move, preferred_element_type=F32)
        hp[i] = out.astype(BF16)
        return 0

    lax.fori_loop(0, AHEAD, spread, 0)
    acc[...] = jnp.zeros_like(acc)
    loads[4].wait()

    lane128 = lax.broadcasted_iota(jnp.int32, (1, 128), 1)

    def score_to(i, k):
        return remote(sc.at[i, k // 2], s1.at[i * NX + x], s1_s, s1_r, (share_of(i) * NX + k, ep))

    def add_pair(i):
        e = share_of(i)

        @pl.when(lax.rem(e, 2) == core)
        def _():
            arrived(sib.at[i], sib_r.at[i])
            both = (own[lax.rem(i, 2)] + sib[i].astype(F32)).astype(BF16)

            @pl.when(e == ep)
            def _():
                rsb[y] = both

            @pl.when(e != ep)
            def _():
                comb[i] = both
                remote(comb.at[i], rsb.at[y], y_s, y_r.at[y], (ctx, e)).start()

    def chunk(i):
        e = share_of(i)
        a = [abuf[i, k].astype(F32).reshape(56, 128) for k in range(NX)]
        b = [bbuf[k, i].astype(F32) for k in range(NX)]
        pad = jnp.zeros((8, 128), F32)
        g0 = jnp.concatenate([v for k in range(NX) for v in (a[k], pad)], axis=0).astype(BF16)
        g1 = jnp.concatenate([v for k in range(NX) for v in (b[k][0:56], pad)], axis=0).astype(BF16)
        g2 = jnp.concatenate([v for k in range(NX) for v in (b[k][56:112], pad)], axis=0).astype(BF16)
        g = jnp.concatenate([g0, g1, g2], axis=1)
        w = jnp.concatenate(
            [jnp.where(lane128 < 64, a[k][CAP:CAP + 1], a[k + 1][CAP:CAP + 1]) for k in (0, 2)], axis=1
        )
        h = hp[i].astype(F32)
        back = lax.dot_general(down_v[...], g, (((1,), (1,)), ((), ())), preferred_element_type=F32)
        score = jnp.sum(h * back, axis=0, keepdims=True)
        sc[i, 0] = score[:, 0:128]
        sc[i, 1] = score[:, 128:256]
        for k in range(NX):
            @pl.when((i != 0) | (x != k))
            def _(k=k):
                score_to(i, k).start()

        @pl.when(i == 0)
        def _():
            s1[x] = jnp.where(x >= 2, score[:, 128:256], score[:, 0:128])

        packed = pack(back)

        @pl.when(lax.rem(e, 2) == core)
        def _():
            own[lax.rem(i, 2)] = packed

        @pl.when(lax.rem(e, 2) != core)
        def _():
            pbuf[i] = packed.astype(BF16)
            remote(pbuf.at[i], sib.at[i], sib_s, sib_r.at[i], sibling).start()

        @pl.when(e == ep)
        def _():
            wshare[...] = jnp.broadcast_to(w, (8, 256))

        acc[...] += jnp.dot((h * w).astype(BF16), g, preferred_element_type=F32)

        @pl.when(i != 0)
        def _():
            add_pair(i - 1)

    def step(i, _):
        @pl.when(i < 16 - AHEAD)
        def _():
            spread(i + AHEAD, 0)

        for k, (d, ops) in enumerate(PLAN):
            @pl.when(i == k)
            def _(k=k, d=d, ops=ops):
                for op in ops:
                    hand_on(*op)
                if d != 0 and leaf(d):
                    arrived(abuf.at[k], az_r.at[k, 0])
                if k == 1:
                    sel_t[...] = sel.T
                    loads[5].wait()
                    top = lax.broadcasted_iota(jnp.int32, (16, 128), 0) == 0
                    qmat[...] = lax.dot_general(
                        probs * (jnp.where(top, 1.0, 0.0) - p0), rw_v[...], (((0,), (0,)), ((), ())),
                        precision=lax.Precision.HIGHEST, preferred_element_type=F32,
                    )

        arrived(bbuf.at[pl.ds(0, 3), i], bx_r.at[i])
        chunk(i)
        return 0

    lax.fori_loop(0, 16, step, 0)
    add_pair(15)

    arrived(s1.at[pl.ds(0, 63)], s1_r)
    s3s[...] = jnp.sum(s1[...], axis=0)
    for d in range(1, NY):
        remote(s3s, s3.at[d], s3_s, s3_r, at_y(d)).start()
    s3[0] = s3s[...]
    grad_down[...] = acc[...].astype(BF16)
    arrived(s3.at[pl.ds(0, NY - 1)], s3_r)
    s4s[...] = jnp.sum(s3[...], axis=0)
    last = remote(s4s, s4, s4_s, s4_r, sibling)
    last.start()

    for d in range(1, NY):
        src = lax.rem(y + NY - d, NY)
        arrived(rsb.at[src], y_r.at[src])
    total = rsb[0].astype(F32)
    for d in range(1, NY):
        total = total + rsb[d].astype(F32)
    total = unpack(total) * wshare[0:1]
    grad_hidden[...] = jnp.concatenate([total[:, 64 * k:64 * k + CAP] for k in range(NX)], axis=1).astype(BF16)

    last.wait()
    scores = s4s[...] + s4[...]
    row = jnp.where(lane128 // 64 == lax.rem(x, 2), scores, 0.0)
    route = jnp.sum(sel_t[...] * row, axis=1, keepdims=True)
    grad_tokens[...] = (route * qmat[...]).astype(BF16)

    sent(abuf.at[0, pl.ds(0, 3)], ax_s)
    sent(abuf.at[pl.ds(0, 15)], az_s)
    sent(bbuf.at[0, pl.ds(0, 15)], bz_s)
    sent(bbuf.at[pl.ds(0, 3)], bx_s)
    sent(pbuf.at[pl.ds(0, 8)], sib_s)
    sent(comb.at[pl.ds(0, 7)], y_s)
    sent(s1.at[pl.ds(0, 63)], s1_s)
    sent(s3.at[pl.ds(0, NY - 1)], s3_s)


def shards(grad_out, logits, expert_ids, hidden_act, down_weight, router_weight):
    dma = pltpu.SemaphoreType.DMA
    return pl.pallas_call(
        kernel,
        out_shape=(
            jax.ShapeDtypeStruct((168, 384), BF16),
            jax.ShapeDtypeStruct((168, 208), BF16),
            jax.ShapeDtypeStruct((128, 384), BF16),
        ),
        in_specs=[pl.BlockSpec(memory_space=pl.ANY)] * 6,
        out_specs=[pl.BlockSpec(memory_space=pltpu.VMEM)] * 3,
        scratch_shapes=[
            pltpu.VMEM((128, 384), BF16),
            pltpu.VMEM((16, 128), F32),
            pltpu.VMEM((4, 128), jnp.int32),
            pltpu.VMEM((168, 3328), BF16),
            pltpu.VMEM((168, 384), BF16),
            pltpu.VMEM((16, 384), F32),
            pltpu.VMEM((16, 168, 256), BF16),
            pltpu.VMEM((16, NX, 7, 8, 128), BF16),
            pltpu.VMEM((NX, 16, 112, 128), BF16),
            pltpu.VMEM((168, 384), F32),
            pltpu.VMEM((2, 144, 256), F32),
            pltpu.VMEM((16, 144, 256), BF16),
            pltpu.VMEM((16, 144, 256), BF16),
            pltpu.VMEM((16, 144, 256), BF16),
            pltpu.VMEM((NY, 144, 256), BF16),
            pltpu.VMEM((8, 256), F32),
            pltpu.VMEM((16, 2, 1, 128), F32),
            pltpu.VMEM((64, 1, 128), F32),
            pltpu.VMEM((1, 128), F32),
            pltpu.VMEM((NY, 1, 128), F32),
            pltpu.VMEM((1, 128), F32),
            pltpu.VMEM((1, 128), F32),
            pltpu.VMEM((128, 128), F32),
            pltpu.VMEM((128, 384), F32),
            dma((6,)),
            dma, dma((NX,)),
            dma, dma((16, NX)),
            dma, dma((16,)),
            dma, dma((16,)),
            dma, dma((16,)),
            dma, dma((NY,)),
            dma, dma,
            dma, dma,
            dma, dma,
        ],
        compiler_params=pltpu.CompilerParams(
            collective_id=0, has_side_effects=True, vmem_limit_bytes=56 << 20
        ),
    )(grad_out, logits.T, expert_ids.T, hidden_act, down_weight, router_weight.T)


def solution(mesh):
    placed = (
        P("ctx", "ep"),
        P("ctx", None),
        P("ctx", None),
        P("ctx", None),
        P("ctx", "ep"),
        P("ep", None),
    )
    return jax.shard_map(
        shards,
        mesh=mesh,
        in_specs=placed,
        out_specs=(P("ctx", "ep"), P("ctx", "ep"), P("ctx", "ep")),
        check_vma=False,
    )
```

```python
import functools

import jax
import jax.numpy as jnp
from jax import lax
from jax.experimental import pallas as pl
from jax.experimental.pallas import tpu as pltpu
from jax.sharding import PartitionSpec as P

MESH = pl.DeviceIdType.MESH
CAP = 52
NZ, NX, NY = 16, 4, 8
PLAN = (
    (0, ((0, 0, 1), (0, 0, 3), (0, 0, 2), (2, -1, 0), (2, 1, 0), (2, -2, 0), (2, 2, 0))),
    (-1, ((1, -2, 0), (1, 2, 0), (1, -2, 1), (1, 2, 1), (1, -2, 3), (1, 2, 3), (1, -2, 2), (1, 2, 2))),
    (1, ((2, -3, 0), (2, 3, 0), (2, -4, 0), (2, 4, 0))),
    (-2, ((1, -4, 0), (1, 4, 0), (1, -4, 1), (1, 4, 1))),
    (2, ((1, -4, 3), (1, 4, 3))),
    (-3, ((1, -4, 2), (1, 4, 2))),
    (3, ((2, -5, 0), (2, -6, 0), (2, 5, 0), (2, 6, 0), (1, -6, 0), (1, 6, 0))),
    (-4, ((1, -6, 1), (1, 6, 1))),
    (4, ((1, -6, 3), (1, 6, 3), (1, -6, 2), (1, 6, 2), (2, -7, 0))),
    (-5, ((2, 7, 0),)),
    (-6, ((2, 8, 0),)),
    (5, ()),
    (6, ()),
    (-7, ()),
    (7, ()),
    (8, ()),
)
DZ = tuple(d for d, _ in PLAN)
AT = {d: i for i, d in enumerate(DZ)}
AT[-8] = AT[8]
HAND = {0: (2, -2, 1, -1), -2: (2, 1), 2: (-2, -1), -4: (2, 1), 4: (-2, -1), -6: (1, 2), 6: (-1,)}
AHEAD = 5
F32, BF16 = jnp.float32, jnp.bfloat16


def pick(index, table):
    out = jnp.int32(table[0])
    for i, v in enumerate(table):
        if i:
            out = jnp.where(index == i, jnp.int32(v), out)
    return out


def pack(v):
    lane = lax.rem(lax.broadcasted_iota(jnp.int32, (144, 256), 1), 64)
    tail = [pltpu.roll(v[144:168], CAP - 12 * c, 1) for c in range(5)]
    tail.append(jnp.zeros((24, 256), F32))
    return jnp.where(lane < CAP, v[0:144], jnp.concatenate(tail, axis=0))


def unpack(v):
    lane = lax.rem(lax.broadcasted_iota(jnp.int32, (24, 256), 1), 64)
    tail = jnp.zeros((24, 256), F32)
    for c in range(5):
        part = pltpu.roll(v[24 * c:24 * c + 24], 256 - (CAP - 12 * c), 1)
        tail = jnp.where((lane >= 12 * c) & (lane < 12 * c + 12), part, tail)
    return jnp.concatenate([v, tail], axis=0)


def kernel(
    grad_out, logits_t, ids_t, hidden, down, router_t,
    grad_down, grad_hidden, grad_tokens,
    go_v, log_v, ids_v, hid_v, down_v, rw_v,
    hp, abuf, bbuf, acc, own, pbuf, sib, comb, rsb, wshare,
    sc, s1, s3s, s3, sel_t, qmat,
    in_sem, ax_s, ax_r, az_s, az_r, bz_s, bz_r, bx_s, bx_r,
    sib_s, sib_r, y_s, y_r, s1_s, s1_r, s3_s, s3_r, known,
):
    ctx, ep = lax.axis_index("ctx"), lax.axis_index("ep")
    z, x = ctx // NX, lax.rem(ctx, NX)
    y, core = ep // 2, lax.rem(ep, 2)

    def at_z(d):
        return (lax.rem(z + d + NZ, NZ) * NX + x, ep)

    def at_x(d):
        return (z * NX + lax.rem(x + d, NX), ep)

    def at_y(d):
        return (ctx, lax.rem(y + d, NY) * 2 + core)

    def from_x(o):
        return lax.rem(x + NX - o, NX)

    sibling = (ctx, y * 2 + 1 - core)

    def remote(src, dst, send, recv, to):
        return pltpu.make_async_remote_copy(
            src_ref=src, dst_ref=dst, send_sem=send, recv_sem=recv, device_id=to, device_id_type=MESH
        )

    def arrived(ref, sem):
        remote(ref, ref, s3_s, sem, sibling).wait_recv()

    def sent(ref, sem):
        remote(ref, ref, sem, s3_r, sibling).wait_send()

    loads = [
        pltpu.make_async_copy(s, d, in_sem.at[i])
        for i, (s, d) in enumerate(
            ((ids_t, ids_v), (grad_out, go_v), (logits_t, log_v), (hidden, hid_v), (down, down_v), (router_t, rw_v))
        )
    ]
    for c in loads:
        c.start()

    barrier = pltpu.get_barrier_semaphore()
    greet = [at_z(d) for d in (2, -2, 1, -1)] + [at_x(d) for d in (2, 1, 3)]
    greet += [at_y(1), at_y(NY - 1), sibling]
    for to in greet:
        pl.semaphore_signal(barrier, inc=1, device_id=to, device_id_type=MESH)

    loads[0].wait()
    named = jnp.max(jnp.where(ids_v[...] == 0, 1.0, 0.0).astype(F32), axis=0, keepdims=True)
    rows = lax.broadcasted_iota(jnp.int32, (128, 128), 0)
    cols = lax.broadcasted_iota(jnp.int32, (128, 128), 1)
    before = jnp.where(rows < cols, 1.0, 0.0).astype(BF16)
    named8 = jnp.broadcast_to(named, (8, 128))
    pos = jnp.dot(named8.astype(BF16), before, preferred_element_type=F32)[0:1]
    slot_row = lax.rem(rows, 64).astype(F32)
    sel = jnp.where((slot_row == pos) & (named > 0.5), 1.0, 0.0).astype(F32)
    sel_bf = sel.astype(BF16)

    loads[2].wait()
    logit = log_v[...]
    grown = jnp.exp(logit - jnp.max(logit, axis=0, keepdims=True))
    probs = grown / jnp.sum(grown, axis=0, keepdims=True)
    p0 = probs[0:1]
    weight = jnp.where(named > 0.5, p0, 0.0).astype(BF16)
    weight_row = lax.dot_general(
        jnp.broadcast_to(weight.astype(F32), (8, 128)).astype(BF16), sel_bf,
        (((1,), (1,)), ((), ())), preferred_element_type=F32,
    )[0:1]

    loads[1].wait()
    slots = jnp.dot(sel_bf[0:64], go_v[...], preferred_element_type=F32)[0:56]
    row56 = lax.broadcasted_iota(jnp.int32, (56, 128), 0)
    first = jnp.where(row56 == CAP, weight_row, slots[:, 0:128])
    abuf[0, x] = first.reshape(7, 8, 128).astype(BF16)
    bbuf[x, 0] = jnp.concatenate([slots[:, 128:256], slots[:, 256:384]], axis=0).astype(BF16)

    pl.semaphore_wait(barrier, len(greet))

    def pass_on(hop):
        if hop > 1:
            pl.semaphore_wait(known.at[hop - 2], 2)
        if hop < NY // 2:
            for to in (at_y(1), at_y(NY - 1)):
                pl.semaphore_signal(known.at[hop - 1], inc=1, device_id=to, device_id_type=MESH)

    def leaf(d):
        return d not in HAND

    def send_a(d, o):
        k = from_x(o)
        for shift in HAND[d]:
            there = d - shift
            if there == -8:
                there = 8
            sem = az_r.at[AT[there], 0 if leaf(there) else o]
            remote(abuf.at[AT[d], k], abuf.at[AT[there], k], az_s, sem, at_z(shift)).start()

    def send_b(d):
        for shift in HAND.get(d, ()):
            there = AT[d - shift]
            remote(bbuf.at[x, AT[d]], bbuf.at[x, there], bz_s, bz_r.at[there], at_z(shift)).start()

    def send_bx(i):
        for o in (1, 3, 2):
            remote(bbuf.at[x, i], bbuf.at[x, i], bx_s, bx_r.at[i], at_x(o)).start()

    for o in (1, 3, 2):
        remote(abuf.at[0, x], abuf.at[0, x], ax_s, ax_r.at[o], at_x(o)).start()
    send_b(0)
    send_a(0, 0)
    send_bx(0)
    pass_on(1)

    def hand_on(op, d, o):
        if op == 0:
            arrived(abuf.at[0, from_x(o)], ax_r.at[o])
            send_a(0, o)
        elif op == 1:
            arrived(abuf.at[AT[d], from_x(o)], az_r.at[AT[d], o])
            send_a(d, o)
        else:
            arrived(bbuf.at[x, AT[d]], bz_r.at[AT[d]])
            send_b(d)
            send_bx(AT[d])

    loads[3].wait()

    def share_of(i):
        return lax.rem(z + pick(i, DZ) + NZ, NZ)

    def spread(i, _):
        start = share_of(i) * (NX * CAP)
        tile = jnp.minimum(start // 128, 23)
        off = start - tile * 128
        r = lax.broadcasted_iota(jnp.int32, (384, 256), 0)
        c = lax.broadcasted_iota(jnp.int32, (384, 256), 1)
        lane = lax.rem(c, 64)
        move = jnp.where((r == off + (c // 64) * CAP + lane) & (lane < CAP), 1.0, 0.0).astype(BF16)
        out = jnp.dot(hid_v[:, pl.ds(pl.multiple_of(tile * 128, 128), 384)], move, preferred_element_type=F32)
        hp[i] = out.astype(BF16)
        return 0

    lax.fori_loop(0, AHEAD, spread, 0)
    acc[...] = jnp.zeros_like(acc)
    loads[4].wait()

    lane128 = lax.broadcasted_iota(jnp.int32, (1, 128), 1)

    def score_to(i, k):
        return remote(sc.at[i, k // 2], s1.at[i * NX + x], s1_s, s1_r, (share_of(i) * NX + k, ep))

    def add_pair(i):
        e = share_of(i)

        @pl.when(lax.rem(e, 2) == core)
        def _():
            arrived(sib.at[i], sib_r.at[i])
            both = (own[lax.rem(i, 2)] + sib[i].astype(F32)).astype(BF16)

            @pl.when(e == ep)
            def _():
                rsb[y] = both

            @pl.when(e != ep)
            def _():
                comb[i] = both
                remote(comb.at[i], rsb.at[y], y_s, y_r.at[y], (ctx, e)).start()

    def chunk(i):
        e = share_of(i)
        a = [abuf[i, k].astype(F32).reshape(56, 128) for k in range(NX)]
        b = [bbuf[k, i].astype(F32) for k in range(NX)]
        pad = jnp.zeros((8, 128), F32)
        g0 = jnp.concatenate([v for k in range(NX) for v in (a[k], pad)], axis=0).astype(BF16)
        g1 = jnp.concatenate([v for k in range(NX) for v in (b[k][0:56], pad)], axis=0).astype(BF16)
        g2 = jnp.concatenate([v for k in range(NX) for v in (b[k][56:112], pad)], axis=0).astype(BF16)
        g = jnp.concatenate([g0, g1, g2], axis=1)
        w = jnp.concatenate(
            [jnp.where(lane128 < 64, a[k][CAP:CAP + 1], a[k + 1][CAP:CAP + 1]) for k in (0, 2)], axis=1
        )
        h = hp[i].astype(F32)
        back = lax.dot_general(down_v[...], g, (((1,), (1,)), ((), ())), preferred_element_type=F32)
        score = jnp.sum(h * back, axis=0, keepdims=True)
        sc[i, 0] = score[:, 0:128]
        sc[i, 1] = score[:, 128:256]
        for k in range(NX):
            @pl.when((i != 0) | (x != k))
            def _(k=k):
                score_to(i, k).start()

        @pl.when(i == 0)
        def _():
            s1[x] = jnp.where(x >= 2, score[:, 128:256], score[:, 0:128])

        packed = pack(back)

        @pl.when(lax.rem(e, 2) == core)
        def _():
            own[lax.rem(i, 2)] = packed

        @pl.when(lax.rem(e, 2) != core)
        def _():
            pbuf[i] = packed.astype(BF16)
            remote(pbuf.at[i], sib.at[i], sib_s, sib_r.at[i], sibling).start()

        @pl.when(e == ep)
        def _():
            wshare[...] = jnp.broadcast_to(w, (8, 256))

        acc[...] += jnp.dot((h * w).astype(BF16), g, preferred_element_type=F32)

        @pl.when(i != 0)
        def _():
            add_pair(i - 1)

    def step(i, _):
        @pl.when(i < 16 - AHEAD)
        def _():
            spread(i + AHEAD, 0)

        for k, (d, ops) in enumerate(PLAN):
            @pl.when(i == k)
            def _(k=k, d=d, ops=ops):
                for n, op in enumerate(ops):
                    if k < 2 and n == 3:
                        pass_on(k + 2)
                    hand_on(*op)
                if d != 0 and leaf(d):
                    arrived(abuf.at[k], az_r.at[k, 0])
                if k == 1:
                    pass_on(4)
                    sel_t[...] = sel.T
                    loads[5].wait()
                    top = lax.broadcasted_iota(jnp.int32, (16, 128), 0) == 0
                    qmat[...] = lax.dot_general(
                        probs * (jnp.where(top, 1.0, 0.0) - p0), rw_v[...], (((0,), (0,)), ((), ())),
                        precision=lax.Precision.HIGHEST, preferred_element_type=F32,
                    )

        arrived(bbuf.at[pl.ds(0, 3), i], bx_r.at[i])
        chunk(i)
        return 0

    lax.fori_loop(0, 16, step, 0)
    add_pair(15)

    arrived(s1.at[pl.ds(0, 63)], s1_r)
    s3s[...] = jnp.sum(s1[...], axis=0)
    for d in (4, 3, 5, 2, 6, 1, 7, 0):
        for other in (0, 1):
            if d or other:
                to = (ctx, lax.rem(y + d, NY) * 2 + (1 - core if other else core))
                remote(s3s, s3.at[2 * d + other], s3_s, s3_r, to).start()
    s3[0] = s3s[...]
    grad_down[...] = acc[...].astype(BF16)

    for d in range(1, NY):
        src = lax.rem(y + NY - d, NY)
        arrived(rsb.at[src], y_r.at[src])
    total = rsb[0].astype(F32)
    for d in range(1, NY):
        total = total + rsb[d].astype(F32)
    total = unpack(total) * wshare[0:1]
    grad_hidden[...] = jnp.concatenate([total[:, 64 * k:64 * k + CAP] for k in range(NX)], axis=1).astype(BF16)

    arrived(s3.at[pl.ds(0, 15)], s3_r)
    row = jnp.where(lane128 // 64 == lax.rem(x, 2), jnp.sum(s3[...], axis=0), 0.0)
    route = jnp.sum(sel_t[...] * row, axis=1, keepdims=True)
    grad_tokens[...] = (route * qmat[...]).astype(BF16)

    sent(abuf.at[0, pl.ds(0, 3)], ax_s)
    sent(abuf.at[pl.ds(0, 15)], az_s)
    sent(bbuf.at[0, pl.ds(0, 15)], bz_s)
    sent(bbuf.at[pl.ds(0, 3)], bx_s)
    sent(pbuf.at[pl.ds(0, 8)], sib_s)
    sent(comb.at[pl.ds(0, 7)], y_s)
    sent(s1.at[pl.ds(0, 63)], s1_s)
    sent(s3.at[pl.ds(0, 15)], s3_s)


def copy_out(a, b, c, a_out, b_out, c_out, sem):
    copies = [
        pltpu.make_async_copy(v, o, sem.at[i]) for i, (v, o) in enumerate(((a, a_out), (b, b_out), (c, c_out)))
    ]
    for v in copies:
        v.start()
    for v in copies:
        v.wait()


def shards(grad_out, logits, expert_ids, hidden_act, down_weight, router_weight):
    dma = pltpu.SemaphoreType.DMA
    results = pl.pallas_call(
        kernel,
        out_shape=(
            pltpu.VMEM((168, 384), BF16),
            pltpu.VMEM((168, 208), BF16),
            pltpu.VMEM((128, 384), BF16),
        ),
        in_specs=[pl.BlockSpec(memory_space=pl.ANY)] * 6,
        out_specs=[pl.BlockSpec(memory_space=pltpu.VMEM)] * 3,
        scratch_shapes=[
            pltpu.VMEM((128, 384), BF16),
            pltpu.VMEM((16, 128), F32),
            pltpu.VMEM((4, 128), jnp.int32),
            pltpu.VMEM((168, 3328), BF16),
            pltpu.VMEM((168, 384), BF16),
            pltpu.VMEM((16, 384), F32),
            pltpu.VMEM((16, 168, 256), BF16),
            pltpu.VMEM((16, NX, 7, 8, 128), BF16),
            pltpu.VMEM((NX, 16, 112, 128), BF16),
            pltpu.VMEM((168, 384), F32),
            pltpu.VMEM((2, 144, 256), F32),
            pltpu.VMEM((16, 144, 256), BF16),
            pltpu.VMEM((16, 144, 256), BF16),
            pltpu.VMEM((16, 144, 256), BF16),
            pltpu.VMEM((NY, 144, 256), BF16),
            pltpu.VMEM((8, 256), F32),
            pltpu.VMEM((16, 2, 1, 128), F32),
            pltpu.VMEM((64, 1, 128), F32),
            pltpu.VMEM((1, 128), F32),
            pltpu.VMEM((16, 1, 128), F32),
            pltpu.VMEM((128, 128), F32),
            pltpu.VMEM((128, 384), F32),
            dma((6,)),
            dma, dma((NX,)),
            dma, dma((16, NX)),
            dma, dma((16,)),
            dma, dma((16,)),
            dma, dma((16,)),
            dma, dma((NY,)),
            dma, dma,
            dma, dma,
            pltpu.SemaphoreType.REGULAR((3,)),
        ],
        compiler_params=pltpu.CompilerParams(
            collective_id=0, has_side_effects=True, vmem_limit_bytes=56 << 20
        ),
    )(grad_out, logits.T, expert_ids.T, hidden_act, down_weight, router_weight.T)
    return pl.pallas_call(
        copy_out,
        out_shape=tuple(jax.ShapeDtypeStruct(r.shape, r.dtype) for r in results),
        in_specs=[pl.BlockSpec(memory_space=pltpu.VMEM)] * 3,
        out_specs=[pl.BlockSpec(memory_space=pl.ANY)] * 3,
        scratch_shapes=[dma((3,))],
    )(*(pltpu.with_memory_space_constraint(r, pltpu.VMEM) for r in results))


def solution(mesh):
    placed = (
        P("ctx", "ep"),
        P("ctx", None),
        P("ctx", None),
        P("ctx", None),
        P("ctx", "ep"),
        P("ep", None),
    )
    return jax.shard_map(
        shards,
        mesh=mesh,
        in_specs=placed,
        out_specs=(P("ctx", "ep"), P("ctx", "ep"), P("ctx", "ep")),
        check_vma=False,
    )
```

```python
import functools

import jax
import jax.numpy as jnp
from jax import lax
from jax.experimental import pallas as pl
from jax.experimental.pallas import tpu as pltpu
from jax.sharding import PartitionSpec as P

MESH = pl.DeviceIdType.MESH
CAP = 52
NZ, NX, NY = 16, 4, 8
PLAN = (
    (0, ((0, 0, 1), (0, 0, 3), (0, 0, 2), (2, -1, 0), (2, 1, 0), (2, -2, 0), (2, 2, 0))),
    (-1, ((1, -2, 0), (1, 2, 0), (1, -2, 1), (1, 2, 1), (1, -2, 3), (1, 2, 3), (1, -2, 2), (1, 2, 2))),
    (1, ((2, -3, 0), (2, 3, 0), (2, -4, 0), (2, 4, 0))),
    (-2, ((1, -4, 0), (1, 4, 0), (1, -4, 1), (1, 4, 1))),
    (2, ((1, -4, 3), (1, 4, 3), (1, -4, 2), (1, 4, 2))),
    (-3, ((2, -5, 0),)),
    (-4, ((2, -6, 0), (2, 5, 0), (2, 6, 0), (1, -6, 0), (1, 6, 0), (1, -6, 1), (1, 6, 1))),
    (4, ((1, -6, 3), (1, 6, 3))),
    (-5, ((1, -6, 2), (1, 6, 2), (2, -7, 0), (2, 7, 0))),
    (-6, ((2, 8, 0),)),
    (5, ()),
    (6, ()),
    (3, ()),
    (-7, ()),
    (7, ()),
    (8, ()),
)
DZ = tuple(d for d, _ in PLAN)
AT = {d: i for i, d in enumerate(DZ)}
AT[-8] = AT[8]
HAND = {0: (2, -2, 1, -1), -2: (2, 1), 2: (-2, -1), -4: (2, 1), 4: (-2, -1), -6: (1, 2), 6: (-1,)}
AHEAD = 5
F32, BF16 = jnp.float32, jnp.bfloat16


def pick(index, table):
    out = jnp.int32(table[0])
    for i, v in enumerate(table):
        if i:
            out = jnp.where(index == i, jnp.int32(v), out)
    return out


def pack(v):
    lane = lax.rem(lax.broadcasted_iota(jnp.int32, (144, 256), 1), 64)
    tail = [pltpu.roll(v[144:168], CAP - 12 * c, 1) for c in range(5)]
    tail.append(jnp.zeros((24, 256), F32))
    return jnp.where(lane < CAP, v[0:144], jnp.concatenate(tail, axis=0))


def unpack(v):
    lane = lax.rem(lax.broadcasted_iota(jnp.int32, (24, 256), 1), 64)
    tail = jnp.zeros((24, 256), F32)
    for c in range(5):
        part = pltpu.roll(v[24 * c:24 * c + 24], 256 - (CAP - 12 * c), 1)
        tail = jnp.where((lane >= 12 * c) & (lane < 12 * c + 12), part, tail)
    return jnp.concatenate([v, tail], axis=0)


def kernel(
    grad_out, logits_t, ids_t, hidden, down, router_t,
    grad_down, grad_hidden, grad_tokens,
    go_v, log_v, ids_v, hid_v, down_v, rw_v,
    hp, abuf, bbuf, acc, own, pbuf, sib, comb, rsb, wshare,
    sc, s1, s3s, s3, sel_t, qmat,
    in_sem, ax_s, ax_r, az_s, az_r, bz_s, bz_r, bx_s, bx_r,
    sib_s, sib_r, y_s, y_r, s1_s, s1_r, s3_s, s3_r, known,
):
    ctx, ep = lax.axis_index("ctx"), lax.axis_index("ep")
    z, x = ctx // NX, lax.rem(ctx, NX)
    y, core = ep // 2, lax.rem(ep, 2)

    def at_z(d):
        return (lax.rem(z + d + NZ, NZ) * NX + x, ep)

    def at_x(d):
        return (z * NX + lax.rem(x + d, NX), ep)

    def at_y(d):
        return (ctx, lax.rem(y + d, NY) * 2 + core)

    def from_x(o):
        return lax.rem(x + NX - o, NX)

    sibling = (ctx, y * 2 + 1 - core)

    def remote(src, dst, send, recv, to):
        return pltpu.make_async_remote_copy(
            src_ref=src, dst_ref=dst, send_sem=send, recv_sem=recv, device_id=to, device_id_type=MESH
        )

    def arrived(ref, sem):
        remote(ref, ref, s3_s, sem, sibling).wait_recv()

    def sent(ref, sem):
        remote(ref, ref, sem, s3_r, sibling).wait_send()

    loads = [
        pltpu.make_async_copy(s, d, in_sem.at[i])
        for i, (s, d) in enumerate(
            ((ids_t, ids_v), (grad_out, go_v), (logits_t, log_v), (hidden, hid_v), (down, down_v), (router_t, rw_v))
        )
    ]
    for c in loads:
        c.start()

    barrier = pltpu.get_barrier_semaphore()
    greet = [at_z(d) for d in (2, -2, 1, -1)] + [at_x(d) for d in (2, 1, 3)]
    greet += [at_y(1), at_y(NY - 1), sibling]
    for to in greet:
        pl.semaphore_signal(barrier, inc=1, device_id=to, device_id_type=MESH)

    loads[0].wait()
    named = jnp.max(jnp.where(ids_v[...] == 0, 1.0, 0.0).astype(F32), axis=0, keepdims=True)
    rows = lax.broadcasted_iota(jnp.int32, (128, 128), 0)
    cols = lax.broadcasted_iota(jnp.int32, (128, 128), 1)
    before = jnp.where(rows < cols, 1.0, 0.0).astype(BF16)
    named8 = jnp.broadcast_to(named, (8, 128))
    pos = jnp.dot(named8.astype(BF16), before, preferred_element_type=F32)[0:1]
    slot_row = lax.rem(rows, 64).astype(F32)
    sel = jnp.where((slot_row == pos) & (named > 0.5), 1.0, 0.0).astype(F32)
    sel_bf = sel.astype(BF16)

    loads[2].wait()
    logit = log_v[...]
    grown = jnp.exp(logit - jnp.max(logit, axis=0, keepdims=True))
    probs = grown / jnp.sum(grown, axis=0, keepdims=True)
    p0 = probs[0:1]
    weight = jnp.where(named > 0.5, p0, 0.0).astype(BF16)
    weight_row = lax.dot_general(
        jnp.broadcast_to(weight.astype(F32), (8, 128)).astype(BF16), sel_bf,
        (((1,), (1,)), ((), ())), preferred_element_type=F32,
    )[0:1]

    loads[1].wait()
    slots = jnp.dot(sel_bf[0:64], go_v[...], preferred_element_type=F32)[0:56]
    row56 = lax.broadcasted_iota(jnp.int32, (56, 128), 0)
    first = jnp.where(row56 == CAP, weight_row, slots[:, 0:128])
    abuf[0, x] = first.reshape(7, 8, 128).astype(BF16)
    rest = jnp.zeros((48, 128), F32)
    upper = jnp.concatenate([slots[:, 128:256], rest], axis=0)
    lower = pltpu.roll(jnp.concatenate([slots[:, 256:384], rest], axis=0), CAP, 0)
    row104 = lax.broadcasted_iota(jnp.int32, (104, 128), 0)
    bbuf[x, 0] = jnp.where(row104 < CAP, upper, lower).reshape(13, 8, 128).astype(BF16)

    pl.semaphore_wait(barrier, len(greet))

    def pass_on(hop):
        if hop > 1:
            pl.semaphore_wait(known.at[hop - 2], 2)
        if hop < NY // 2:
            for to in (at_y(1), at_y(NY - 1)):
                pl.semaphore_signal(known.at[hop - 1], inc=1, device_id=to, device_id_type=MESH)

    def leaf(d):
        return d not in HAND

    def send_a(d, o):
        k = from_x(o)
        for shift in HAND[d]:
            there = d - shift
            if there == -8:
                there = 8
            sem = az_r.at[AT[there], 0 if leaf(there) else o]
            remote(abuf.at[AT[d], k], abuf.at[AT[there], k], az_s, sem, at_z(shift)).start()

    def send_b(d):
        for shift in HAND.get(d, ()):
            there = AT[d - shift]
            remote(bbuf.at[x, AT[d]], bbuf.at[x, there], bz_s, bz_r.at[there], at_z(shift)).start()

    def send_bx(i):
        for o in (1, 3, 2):
            remote(bbuf.at[x, i], bbuf.at[x, i], bx_s, bx_r.at[i], at_x(o)).start()

    for o in (1, 3, 2):
        remote(abuf.at[0, x], abuf.at[0, x], ax_s, ax_r.at[o], at_x(o)).start()
    send_b(0)
    send_a(0, 0)
    send_bx(0)
    pass_on(1)

    def hand_on(op, d, o):
        if op == 0:
            arrived(abuf.at[0, from_x(o)], ax_r.at[o])
            send_a(0, o)
        elif op == 1:
            arrived(abuf.at[AT[d], from_x(o)], az_r.at[AT[d], o])
            send_a(d, o)
        else:
            arrived(bbuf.at[x, AT[d]], bz_r.at[AT[d]])
            send_b(d)
            send_bx(AT[d])

    loads[3].wait()

    def share_of(i):
        return lax.rem(z + pick(i, DZ) + NZ, NZ)

    def spread(i, _):
        start = share_of(i) * (NX * CAP)
        tile = jnp.minimum(start // 128, 23)
        off = start - tile * 128
        r = lax.broadcasted_iota(jnp.int32, (384, 256), 0)
        c = lax.broadcasted_iota(jnp.int32, (384, 256), 1)
        lane = lax.rem(c, 64)
        move = jnp.where((r == off + (c // 64) * CAP + lane) & (lane < CAP), 1.0, 0.0).astype(BF16)
        out = jnp.dot(hid_v[:, pl.ds(pl.multiple_of(tile * 128, 128), 384)], move, preferred_element_type=F32)
        hp[i] = out.astype(BF16)
        return 0

    lax.fori_loop(0, AHEAD, spread, 0)
    acc[...] = jnp.zeros_like(acc)
    loads[4].wait()

    lane128 = lax.broadcasted_iota(jnp.int32, (1, 128), 1)

    def score_to(i, e, k):
        return remote(sc.at[i, k // 2], s1.at[i * NX + x], s1_s, s1_r, (e * NX + k, ep))

    def add_pair(i, e):
        @pl.when(lax.rem(e, 2) == core)
        def _():
            arrived(sib.at[i], sib_r.at[i])
            both = (own[lax.rem(i, 2)] + sib[i].astype(F32)).astype(BF16)

            @pl.when(e == ep)
            def _():
                rsb[y] = both

            @pl.when(e != ep)
            def _():
                comb[i] = both
                remote(comb.at[i], rsb.at[y], y_s, y_r.at[y], (ctx, e)).start()

    def chunk(i, e, before):
        a = [abuf[i, k].astype(F32).reshape(56, 128) for k in range(NX)]
        b = [bbuf[k, i].astype(F32).reshape(104, 128) for k in range(NX)]
        c = [pltpu.roll(v, CAP, 0) for v in b]
        pad = jnp.zeros((8, 128), F32)
        g0 = jnp.concatenate([v for k in range(NX) for v in (a[k], pad)], axis=0).astype(BF16)
        g1 = jnp.concatenate([v for k in range(NX) for v in (b[k][0:56], pad)], axis=0).astype(BF16)
        g2 = jnp.concatenate([v for k in range(NX) for v in (c[k][0:56], pad)], axis=0).astype(BF16)
        g = jnp.concatenate([g0, g1, g2], axis=1)
        w = jnp.concatenate(
            [jnp.where(lane128 < 64, a[k][CAP:CAP + 1], a[k + 1][CAP:CAP + 1]) for k in (0, 2)], axis=1
        )
        h = hp[i].astype(F32)
        back = lax.dot_general(down_v[...], g, (((1,), (1,)), ((), ())), preferred_element_type=F32)
        score = jnp.sum(h * back, axis=0, keepdims=True)
        sc[i, 0] = score[:, 0:128]
        sc[i, 1] = score[:, 128:256]
        for k in range(NX):
            @pl.when((i != 0) | (x != k))
            def _(k=k):
                score_to(i, e, k).start()

        @pl.when(i == 0)
        def _():
            s1[x] = jnp.where(x >= 2, score[:, 128:256], score[:, 0:128])

        packed = pack(back)

        @pl.when(lax.rem(e, 2) == core)
        def _():
            own[lax.rem(i, 2)] = packed

        @pl.when(lax.rem(e, 2) != core)
        def _():
            pbuf[i] = packed.astype(BF16)
            remote(pbuf.at[i], sib.at[i], sib_s, sib_r.at[i], sibling).start()

        @pl.when(e == ep)
        def _():
            wshare[...] = jnp.broadcast_to(w, (8, 256))

        @pl.when(i != 0)
        def _():
            add_pair(i - 1, before)

        acc[...] += jnp.dot((h * w).astype(BF16), g, preferred_element_type=F32)

    def step(i, before):
        @pl.when(i < 16 - AHEAD)
        def _():
            spread(i + AHEAD, 0)

        for k, (d, ops) in enumerate(PLAN):
            @pl.when(i == k)
            def _(k=k, d=d, ops=ops):
                for n, op in enumerate(ops):
                    if k < 2 and n == 3:
                        pass_on(k + 2)
                    hand_on(*op)
                if d != 0 and leaf(d):
                    arrived(abuf.at[k], az_r.at[k, 0])
                if k == 1:
                    pass_on(4)
                    sel_t[...] = sel.T
                    loads[5].wait()
                    top = lax.broadcasted_iota(jnp.int32, (16, 128), 0) == 0
                    qmat[...] = lax.dot_general(
                        probs * (jnp.where(top, 1.0, 0.0) - p0), rw_v[...], (((0,), (0,)), ((), ())),
                        precision=lax.Precision.HIGHEST, preferred_element_type=F32,
                    )

        arrived(bbuf.at[pl.ds(0, 3), i], bx_r.at[i])
        e = share_of(i)
        chunk(i, e, before)
        return e

    final = lax.fori_loop(0, 16, step, jnp.int32(0))
    add_pair(15, final)

    arrived(s1.at[pl.ds(0, 63)], s1_r)
    s3s[...] = jnp.sum(s1[...], axis=0)
    for d in (4, 3, 5, 2, 6, 1, 7, 0):
        for other in (0, 1):
            if d or other:
                to = (ctx, lax.rem(y + d, NY) * 2 + (1 - core if other else core))
                remote(s3s, s3.at[2 * d + other], s3_s, s3_r, to).start()
    s3[0] = s3s[...]
    grad_down[...] = acc[...].astype(BF16)

    for d in range(1, NY):
        src = lax.rem(y + NY - d, NY)
        arrived(rsb.at[src], y_r.at[src])
    total = rsb[0].astype(F32)
    for d in range(1, NY):
        total = total + rsb[d].astype(F32)
    total = unpack(total) * wshare[0:1]
    grad_hidden[...] = jnp.concatenate([total[:, 64 * k:64 * k + CAP] for k in range(NX)], axis=1).astype(BF16)

    arrived(s3.at[pl.ds(0, 15)], s3_r)
    row = jnp.where(lane128 // 64 == lax.rem(x, 2), jnp.sum(s3[...], axis=0), 0.0)
    route = jnp.sum(sel_t[...] * row, axis=1, keepdims=True)
    grad_tokens[...] = (route * qmat[...]).astype(BF16)

    sent(abuf.at[0, pl.ds(0, 3)], ax_s)
    sent(abuf.at[pl.ds(0, 15)], az_s)
    sent(bbuf.at[0, pl.ds(0, 15)], bz_s)
    sent(bbuf.at[pl.ds(0, 3)], bx_s)
    sent(pbuf.at[pl.ds(0, 8)], sib_s)
    sent(comb.at[pl.ds(0, 7)], y_s)
    sent(s1.at[pl.ds(0, 63)], s1_s)
    sent(s3.at[pl.ds(0, 15)], s3_s)


def copy_out(a, b, c, a_out, b_out, c_out, sem):
    copies = [
        pltpu.make_async_copy(v, o, sem.at[i]) for i, (v, o) in enumerate(((a, a_out), (b, b_out), (c, c_out)))
    ]
    for v in copies:
        v.start()
    for v in copies:
        v.wait()


def shards(grad_out, logits, expert_ids, hidden_act, down_weight, router_weight):
    dma = pltpu.SemaphoreType.DMA
    results = pl.pallas_call(
        kernel,
        out_shape=(
            pltpu.VMEM((168, 384), BF16),
            pltpu.VMEM((168, 208), BF16),
            pltpu.VMEM((128, 384), BF16),
        ),
        in_specs=[pl.BlockSpec(memory_space=pl.ANY)] * 6,
        out_specs=[pl.BlockSpec(memory_space=pltpu.VMEM)] * 3,
        scratch_shapes=[
            pltpu.VMEM((128, 384), BF16),
            pltpu.VMEM((16, 128), F32),
            pltpu.VMEM((4, 128), jnp.int32),
            pltpu.VMEM((168, 3328), BF16),
            pltpu.VMEM((168, 384), BF16),
            pltpu.VMEM((16, 384), F32),
            pltpu.VMEM((16, 168, 256), BF16),
            pltpu.VMEM((16, NX, 7, 8, 128), BF16),
            pltpu.VMEM((NX, 16, 13, 8, 128), BF16),
            pltpu.VMEM((168, 384), F32),
            pltpu.VMEM((2, 144, 256), F32),
            pltpu.VMEM((16, 144, 256), BF16),
            pltpu.VMEM((16, 144, 256), BF16),
            pltpu.VMEM((16, 144, 256), BF16),
            pltpu.VMEM((NY, 144, 256), BF16),
            pltpu.VMEM((8, 256), F32),
            pltpu.VMEM((16, 2, 1, 128), F32),
            pltpu.VMEM((64, 1, 128), F32),
            pltpu.VMEM((1, 128), F32),
            pltpu.VMEM((16, 1, 128), F32),
            pltpu.VMEM((128, 128), F32),
            pltpu.VMEM((128, 384), F32),
            dma((6,)),
            dma, dma((NX,)),
            dma, dma((16, NX)),
            dma, dma((16,)),
            dma, dma((16,)),
            dma, dma((16,)),
            dma, dma((NY,)),
            dma, dma,
            dma, dma,
            pltpu.SemaphoreType.REGULAR((3,)),
        ],
        compiler_params=pltpu.CompilerParams(
            collective_id=0, has_side_effects=True, vmem_limit_bytes=56 << 20
        ),
    )(grad_out, logits.T, expert_ids.T, hidden_act, down_weight, router_weight.T)
    return pl.pallas_call(
        copy_out,
        out_shape=tuple(jax.ShapeDtypeStruct(r.shape, r.dtype) for r in results),
        in_specs=[pl.BlockSpec(memory_space=pltpu.VMEM)] * 3,
        out_specs=[pl.BlockSpec(memory_space=pl.ANY)] * 3,
        scratch_shapes=[dma((3,))],
    )(*(pltpu.with_memory_space_constraint(r, pltpu.VMEM) for r in results))


def solution(mesh):
    placed = (
        P("ctx", "ep"),
        P("ctx", None),
        P("ctx", None),
        P("ctx", None),
        P("ctx", "ep"),
        P("ep", None),
    )
    return jax.shard_map(
        shards,
        mesh=mesh,
        in_specs=placed,
        out_specs=(P("ctx", "ep"), P("ctx", "ep"), P("ctx", "ep")),
        check_vma=False,
    )
```

```python
import functools

import jax
import jax.numpy as jnp
from jax import lax
from jax.experimental import pallas as pl
from jax.experimental.pallas import tpu as pltpu
from jax.sharding import PartitionSpec as P

MESH = pl.DeviceIdType.MESH
CAP = 52
NZ, NX, NY = 16, 4, 8
PLAN = (
    (0, ((0, 0, 1), (0, 0, 3), (0, 0, 2), (2, -1, 0), (2, 1, 0), (2, -2, 0), (2, 2, 0))),
    (-1, ((1, -2, 0), (1, 2, 0), (1, -2, 1), (1, 2, 1), (1, -2, 3), (1, 2, 3), (1, -2, 2), (1, 2, 2))),
    (1, ((2, -3, 0), (2, 3, 0), (2, -4, 0), (2, 4, 0))),
    (-2, ((1, -4, 0), (1, 4, 0), (1, -4, 1), (1, 4, 1))),
    (2, ((1, -4, 3), (1, 4, 3), (1, -4, 2), (1, 4, 2))),
    (-3, ((2, -5, 0),)),
    (-4, ((2, -6, 0), (2, 5, 0), (2, 6, 0), (1, -6, 0), (1, 6, 0), (1, -6, 1), (1, 6, 1))),
    (4, ((1, -6, 3), (1, 6, 3))),
    (-5, ((1, -6, 2), (1, 6, 2), (2, -7, 0), (2, 7, 0))),
    (-6, ((2, 8, 0),)),
    (5, ()),
    (6, ()),
    (3, ()),
    (-7, ()),
    (7, ()),
    (8, ()),
)
DZ = tuple(d for d, _ in PLAN)
AT = {d: i for i, d in enumerate(DZ)}
AT[-8] = AT[8]
HAND = {0: (2, -2, 1, -1), -2: (2, 1), 2: (-2, -1), -4: (2, 1), 4: (-2, -1), -6: (1, 2), 6: (-1,)}
AHEAD = 5
F32, BF16 = jnp.float32, jnp.bfloat16


def pick(index, table):
    out = jnp.int32(table[0])
    for i, v in enumerate(table):
        if i:
            out = jnp.where(index == i, jnp.int32(v), out)
    return out


def pack(v):
    lane = jnp.broadcast_to(lax.rem(lax.broadcasted_iota(jnp.int32, (1, 256), 1), 64), (144, 256))
    tail = [pltpu.roll(v[144:168], CAP - 12 * c, 1) for c in range(5)]
    tail.append(jnp.zeros((24, 256), F32))
    return jnp.where(lane < CAP, v[0:144], jnp.concatenate(tail, axis=0))


def unpack(v):
    lane = jnp.broadcast_to(lax.rem(lax.broadcasted_iota(jnp.int32, (1, 256), 1), 64), (24, 256))
    tail = jnp.zeros((24, 256), F32)
    for c in range(5):
        part = pltpu.roll(v[24 * c:24 * c + 24], 256 - (CAP - 12 * c), 1)
        tail = jnp.where((lane >= 12 * c) & (lane < 12 * c + 12), part, tail)
    return jnp.concatenate([v, tail], axis=0)


def kernel(
    grad_out, logits_t, ids_t, hidden, down, router_t,
    grad_down, grad_hidden, grad_tokens,
    go_v, log_v, ids_v, hid_v, down_v, rw_v,
    hp, abuf, bbuf, acc, own, pbuf, sib, comb, rsb, wshare,
    sc, s1, s3s, s3, sel_t, qmat,
    in_sem, ax_s, ax_r, az_s, az_r, bz_s, bz_r, bx_s, bx_r,
    sib_s, sib_r, y_s, y_r, s1_s, s1_r, s3_s, s3_r, known,
):
    ctx, ep = lax.axis_index("ctx"), lax.axis_index("ep")
    z, x = ctx // NX, lax.rem(ctx, NX)
    y, core = ep // 2, lax.rem(ep, 2)

    def at_z(d):
        return (lax.rem(z + d + NZ, NZ) * NX + x, ep)

    def at_x(d):
        return (z * NX + lax.rem(x + d, NX), ep)

    def at_y(d):
        return (ctx, lax.rem(y + d, NY) * 2 + core)

    def from_x(o):
        return lax.rem(x + NX - o, NX)

    sibling = (ctx, y * 2 + 1 - core)

    def remote(src, dst, send, recv, to):
        return pltpu.make_async_remote_copy(
            src_ref=src, dst_ref=dst, send_sem=send, recv_sem=recv, device_id=to, device_id_type=MESH
        )

    def arrived(ref, sem):
        remote(ref, ref, s3_s, sem, sibling).wait_recv()

    def sent(ref, sem):
        remote(ref, ref, sem, s3_r, sibling).wait_send()

    loads = [
        pltpu.make_async_copy(s, d, in_sem.at[i])
        for i, (s, d) in enumerate(
            ((ids_t, ids_v), (grad_out, go_v), (logits_t, log_v), (hidden, hid_v), (down, down_v), (router_t, rw_v))
        )
    ]
    for c in loads:
        c.start()

    barrier = pltpu.get_barrier_semaphore()
    greet = [at_z(d) for d in (2, -2, 1, -1)] + [at_x(d) for d in (2, 1, 3)]
    greet += [at_y(1), at_y(NY - 1), sibling]
    for to in greet:
        pl.semaphore_signal(barrier, inc=1, device_id=to, device_id_type=MESH)

    loads[0].wait()
    named = jnp.max(jnp.where(ids_v[...] == 0, 1.0, 0.0).astype(F32), axis=0, keepdims=True)
    rows = lax.broadcasted_iota(jnp.int32, (128, 128), 0)
    cols = lax.broadcasted_iota(jnp.int32, (128, 128), 1)
    before = jnp.where(rows < cols, 1.0, 0.0).astype(BF16)
    named8 = jnp.broadcast_to(named, (8, 128))
    pos = jnp.dot(named8.astype(BF16), before, preferred_element_type=F32)[0:1]
    slot_row = lax.rem(rows, 64).astype(F32)
    sel = jnp.where((slot_row == pos) & (named > 0.5), 1.0, 0.0).astype(F32)
    sel_bf = sel.astype(BF16)

    loads[2].wait()
    logit = log_v[...]
    grown = jnp.exp(logit - jnp.max(logit, axis=0, keepdims=True))
    probs = grown / jnp.sum(grown, axis=0, keepdims=True)
    p0 = probs[0:1]
    weight = jnp.where(named > 0.5, p0, 0.0).astype(BF16)
    weight_row = lax.dot_general(
        jnp.broadcast_to(weight.astype(F32), (8, 128)).astype(BF16), sel_bf,
        (((1,), (1,)), ((), ())), preferred_element_type=F32,
    )[0:1]

    loads[1].wait()
    slots = jnp.dot(sel_bf[0:64], go_v[...], preferred_element_type=F32)[0:56]
    row56 = lax.broadcasted_iota(jnp.int32, (56, 128), 0)
    first = jnp.where(row56 == CAP, weight_row, slots[:, 0:128])
    abuf[0, x] = first.reshape(7, 8, 128).astype(BF16)
    rest = jnp.zeros((48, 128), F32)
    upper = jnp.concatenate([slots[:, 128:256], rest], axis=0)
    lower = pltpu.roll(jnp.concatenate([slots[:, 256:384], rest], axis=0), CAP, 0)
    row104 = lax.broadcasted_iota(jnp.int32, (104, 128), 0)
    bbuf[x, 0] = jnp.where(row104 < CAP, upper, lower).reshape(13, 8, 128).astype(BF16)

    pl.semaphore_wait(barrier, len(greet))

    def pass_on(hop):
        if hop > 1:
            pl.semaphore_wait(known.at[hop - 2], 2)
        if hop < NY // 2:
            for to in (at_y(1), at_y(NY - 1)):
                pl.semaphore_signal(known.at[hop - 1], inc=1, device_id=to, device_id_type=MESH)

    def leaf(d):
        return d not in HAND

    def send_a(d, o):
        k = from_x(o)
        for shift in HAND[d]:
            there = d - shift
            if there == -8:
                there = 8
            sem = az_r.at[AT[there], 0 if leaf(there) else o]
            remote(abuf.at[AT[d], k], abuf.at[AT[there], k], az_s, sem, at_z(shift)).start()

    def send_b(d):
        for shift in HAND.get(d, ()):
            there = AT[d - shift]
            remote(bbuf.at[x, AT[d]], bbuf.at[x, there], bz_s, bz_r.at[there], at_z(shift)).start()

    def send_bx(i):
        for o in (1, 3, 2):
            remote(bbuf.at[x, i], bbuf.at[x, i], bx_s, bx_r.at[i], at_x(o)).start()

    for o in (1, 3, 2):
        remote(abuf.at[0, x], abuf.at[0, x], ax_s, ax_r.at[o], at_x(o)).start()
    send_b(0)
    send_a(0, 0)
    send_bx(0)
    pass_on(1)

    def hand_on(op, d, o):
        if op == 0:
            arrived(abuf.at[0, from_x(o)], ax_r.at[o])
            send_a(0, o)
        elif op == 1:
            arrived(abuf.at[AT[d], from_x(o)], az_r.at[AT[d], o])
            send_a(d, o)
        else:
            arrived(bbuf.at[x, AT[d]], bz_r.at[AT[d]])
            send_b(d)
            send_bx(AT[d])

    loads[3].wait()

    def share_of(i):
        return lax.rem(z + pick(i, DZ) + NZ, NZ)

    def spread(i, _):
        start = share_of(i) * (NX * CAP)
        tile = jnp.minimum(start // 128, 23)
        off = start - tile * 128
        r = lax.broadcasted_iota(jnp.int32, (384, 256), 0)
        c = lax.broadcasted_iota(jnp.int32, (1, 256), 1)
        lane = lax.rem(c, 64)
        wanted = jnp.where(lane < CAP, off + (c // 64) * CAP + lane, -1)
        move = jnp.where(r == wanted, 1.0, 0.0).astype(BF16)
        out = jnp.dot(hid_v[:, pl.ds(pl.multiple_of(tile * 128, 128), 384)], move, preferred_element_type=F32)
        hp[i] = out.astype(BF16)
        return 0

    lax.fori_loop(0, AHEAD, spread, 0)
    acc[...] = jnp.zeros_like(acc)
    loads[4].wait()

    lane128 = lax.broadcasted_iota(jnp.int32, (1, 128), 1)

    def score_to(i, e, k):
        return remote(sc.at[i, k // 2], s1.at[i * NX + x], s1_s, s1_r, (e * NX + k, ep))

    def add_pair(i, e):
        @pl.when(lax.rem(e, 2) == core)
        def _():
            arrived(sib.at[i], sib_r.at[i])
            both = (own[lax.rem(i, 2)] + sib[i].astype(F32)).astype(BF16)

            @pl.when(e == ep)
            def _():
                rsb[y] = both

            @pl.when(e != ep)
            def _():
                comb[i] = both
                remote(comb.at[i], rsb.at[y], y_s, y_r.at[y], (ctx, e)).start()

    def chunk(i, e, before):
        a = [abuf[i, k].astype(F32).reshape(56, 128) for k in range(NX)]
        b = [bbuf[k, i].astype(F32).reshape(104, 128) for k in range(NX)]
        c = [pltpu.roll(v, CAP, 0) for v in b]
        pad = jnp.zeros((8, 128), F32)
        g0 = jnp.concatenate([v for k in range(NX) for v in (a[k], pad)], axis=0).astype(BF16)
        g1 = jnp.concatenate([v for k in range(NX) for v in (b[k][0:56], pad)], axis=0).astype(BF16)
        g2 = jnp.concatenate([v for k in range(NX) for v in (c[k][0:56], pad)], axis=0).astype(BF16)
        g = jnp.concatenate([g0, g1, g2], axis=1)
        w = jnp.concatenate(
            [jnp.where(lane128 < 64, a[k][CAP:CAP + 1], a[k + 1][CAP:CAP + 1]) for k in (0, 2)], axis=1
        )
        h = hp[i].astype(F32)
        back = lax.dot_general(down_v[...], g, (((1,), (1,)), ((), ())), preferred_element_type=F32)
        score = jnp.sum(h * back, axis=0, keepdims=True)
        sc[i, 0] = score[:, 0:128]
        sc[i, 1] = score[:, 128:256]
        for k in range(NX):
            @pl.when((i != 0) | (x != k))
            def _(k=k):
                score_to(i, e, k).start()

        @pl.when(i == 0)
        def _():
            s1[x] = jnp.where(x >= 2, score[:, 128:256], score[:, 0:128])

        packed = pack(back)

        @pl.when(lax.rem(e, 2) == core)
        def _():
            own[lax.rem(i, 2)] = packed

        @pl.when(lax.rem(e, 2) != core)
        def _():
            pbuf[i] = packed.astype(BF16)
            remote(pbuf.at[i], sib.at[i], sib_s, sib_r.at[i], sibling).start()

        @pl.when(e == ep)
        def _():
            wshare[...] = jnp.broadcast_to(w, (8, 256))

        @pl.when(i != 0)
        def _():
            add_pair(i - 1, before)

        acc[...] += jnp.dot((h * w).astype(BF16), g, preferred_element_type=F32)

    def step(i, before):
        @pl.when(i < 16 - AHEAD)
        def _():
            spread(i + AHEAD, 0)

        for k, (d, ops) in enumerate(PLAN):
            @pl.when(i == k)
            def _(k=k, d=d, ops=ops):
                for n, op in enumerate(ops):
                    if k < 2 and n == 3:
                        pass_on(k + 2)
                    hand_on(*op)
                if d != 0 and leaf(d):
                    arrived(abuf.at[k], az_r.at[k, 0])
                if k == 1:
                    pass_on(4)
                    sel_t[...] = sel.T
                    loads[5].wait()
                    top = lax.broadcasted_iota(jnp.int32, (16, 128), 0) == 0
                    qmat[...] = lax.dot_general(
                        probs * (jnp.where(top, 1.0, 0.0) - p0), rw_v[...], (((0,), (0,)), ((), ())),
                        precision=lax.Precision.HIGHEST, preferred_element_type=F32,
                    )

        arrived(bbuf.at[pl.ds(0, 3), i], bx_r.at[i])
        e = share_of(i)
        chunk(i, e, before)
        return e

    final = lax.fori_loop(0, 16, step, jnp.int32(0))
    add_pair(15, final)

    arrived(s1.at[pl.ds(0, 63)], s1_r)
    s3s[...] = jnp.sum(s1[...], axis=0)
    for d in (4, 3, 5, 2, 6, 1, 7, 0):
        for other in (0, 1):
            if d or other:
                to = (ctx, lax.rem(y + d, NY) * 2 + (1 - core if other else core))
                remote(s3s, s3.at[2 * d + other], s3_s, s3_r, to).start()
    s3[0] = s3s[...]
    grad_down[...] = acc[...].astype(BF16)

    for d in range(1, NY):
        src = lax.rem(y + NY - d, NY)
        arrived(rsb.at[src], y_r.at[src])
    total = rsb[0].astype(F32)
    for d in range(1, NY):
        total = total + rsb[d].astype(F32)
    total = unpack(total) * wshare[0:1]
    grad_hidden[...] = jnp.concatenate([total[:, 64 * k:64 * k + CAP] for k in range(NX)], axis=1).astype(BF16)

    arrived(s3.at[pl.ds(0, 15)], s3_r)
    row = jnp.where(lane128 // 64 == lax.rem(x, 2), jnp.sum(s3[...], axis=0), 0.0)
    route = jnp.sum(sel_t[...] * row, axis=1, keepdims=True)
    grad_tokens[...] = (route * qmat[...]).astype(BF16)

    sent(abuf.at[0, pl.ds(0, 3)], ax_s)
    sent(abuf.at[pl.ds(0, 15)], az_s)
    sent(bbuf.at[0, pl.ds(0, 15)], bz_s)
    sent(bbuf.at[pl.ds(0, 3)], bx_s)
    sent(pbuf.at[pl.ds(0, 8)], sib_s)
    sent(comb.at[pl.ds(0, 7)], y_s)
    sent(s1.at[pl.ds(0, 63)], s1_s)
    sent(s3.at[pl.ds(0, 15)], s3_s)


def copy_out(a, b, c, a_out, b_out, c_out, sem):
    copies = [
        pltpu.make_async_copy(v, o, sem.at[i]) for i, (v, o) in enumerate(((a, a_out), (b, b_out), (c, c_out)))
    ]
    for v in copies:
        v.start()
    for v in copies:
        v.wait()


def shards(grad_out, logits, expert_ids, hidden_act, down_weight, router_weight):
    dma = pltpu.SemaphoreType.DMA
    results = pl.pallas_call(
        kernel,
        out_shape=(
            pltpu.VMEM((168, 384), BF16),
            pltpu.VMEM((168, 208), BF16),
            pltpu.VMEM((128, 384), BF16),
        ),
        in_specs=[pl.BlockSpec(memory_space=pl.ANY)] * 6,
        out_specs=[pl.BlockSpec(memory_space=pltpu.VMEM)] * 3,
        scratch_shapes=[
            pltpu.VMEM((128, 384), BF16),
            pltpu.VMEM((16, 128), F32),
            pltpu.VMEM((4, 128), jnp.int32),
            pltpu.VMEM((168, 3328), BF16),
            pltpu.VMEM((168, 384), BF16),
            pltpu.VMEM((16, 384), F32),
            pltpu.VMEM((16, 168, 256), BF16),
            pltpu.VMEM((16, NX, 7, 8, 128), BF16),
            pltpu.VMEM((NX, 16, 13, 8, 128), BF16),
            pltpu.VMEM((168, 384), F32),
            pltpu.VMEM((2, 144, 256), F32),
            pltpu.VMEM((16, 144, 256), BF16),
            pltpu.VMEM((16, 144, 256), BF16),
            pltpu.VMEM((16, 144, 256), BF16),
            pltpu.VMEM((NY, 144, 256), BF16),
            pltpu.VMEM((8, 256), F32),
            pltpu.VMEM((16, 2, 1, 128), F32),
            pltpu.VMEM((64, 1, 128), F32),
            pltpu.VMEM((1, 128), F32),
            pltpu.VMEM((16, 1, 128), F32),
            pltpu.VMEM((128, 128), F32),
            pltpu.VMEM((128, 384), F32),
            dma((6,)),
            dma, dma((NX,)),
            dma, dma((16, NX)),
            dma, dma((16,)),
            dma, dma((16,)),
            dma, dma((16,)),
            dma, dma((NY,)),
            dma, dma,
            dma, dma,
            pltpu.SemaphoreType.REGULAR((3,)),
        ],
        compiler_params=pltpu.CompilerParams(
            collective_id=0, has_side_effects=True, vmem_limit_bytes=56 << 20
        ),
    )(grad_out, logits.T, expert_ids.T, hidden_act, down_weight, router_weight.T)
    return pl.pallas_call(
        copy_out,
        out_shape=tuple(jax.ShapeDtypeStruct(r.shape, r.dtype) for r in results),
        in_specs=[pl.BlockSpec(memory_space=pltpu.VMEM)] * 3,
        out_specs=[pl.BlockSpec(memory_space=pl.ANY)] * 3,
        scratch_shapes=[dma((3,))],
    )(*(pltpu.with_memory_space_constraint(r, pltpu.VMEM) for r in results))


def solution(mesh):
    placed = (
        P("ctx", "ep"),
        P("ctx", None),
        P("ctx", None),
        P("ctx", None),
        P("ctx", "ep"),
        P("ep", None),
    )
    return jax.shard_map(
        shards,
        mesh=mesh,
        in_specs=placed,
        out_specs=(P("ctx", "ep"), P("ctx", "ep"), P("ctx", "ep")),
        check_vma=False,
    )
```
